256 devices in a mesh: role: 2 (over core), grp: 8 (over z_hi, y), tp: 16 (over z_lo, x).
Axes of the slice: x: 4, y: 4, z: 8 (z_hi: 2, z_lo: 4; z = z_hi * 4 + z_lo), core: 2. Of those that a mesh axis runs over, the one named last changes fastest.
Arguments:
- residual: bfloat16 [2, 1024, 3584], P('role', 'grp', 'tp'), may hold values from -300 to 300
- queries: bfloat16 [2, 1024, 4096], P('role', 'grp', 'tp'), may hold values from -200 to 200
- kv_cache: bfloat16 [2, 1024, 16, 256], P('role', 'grp'), may hold values from -8 to 8
- cache_lengths: int32 [2, 1024], P('role', 'grp'), may hold values from 2 to 16, as said below
- out_proj: bfloat16 [4096, 3584], P('tp'), may hold values from -0.125 to 0.125
- norm_gain: bfloat16 [3584], replicated, may hold values from 0.099609375 to 1.8984375
- routes: int32 [2, 1024, 3], P('role', 'grp'), may hold values from 0 to 31, all different within a row; in each aligned block of 128 rows (0 to 127, 128 to 255, ..., all dimensions but the last counted through in order) at most 24 rows name the same one
- gate_weights: float32 [2, 1024, 3], P('role', 'grp'), may hold values from 0.2 to 1
- expert_in: bfloat16 [32, 2, 2560, 3584], P(('role', 'grp'), None, 'tp'), may hold values from -0.09375 to 0.09375
- expert_out: bfloat16 [32, 2560, 3584], P(('role', 'grp'), 'tp'), may hold values from -0.15625 to 0.15625
- shared_in: bfloat16 [2, 2560, 3584], P(None, 'tp'), may hold values from -0.09375 to 0.09375
- shared_out: bfloat16 [2560, 3584], P('tp'), may hold values from -0.15625 to 0.15625
Outputs:
- layer_out: bfloat16 [2, 1024, 3584], P('role', 'grp', 'tp')
The draws below stay inside these ranges and needn't reach their ends.
Inputs may be any that keep to these rules, and one draw needn't show every extreme that they name: `routes`: each row names 3 different experts. In every aligned block of 128 rows of one micro-batch (the rows of one data group) no expert is named by more than 24 rows, and in some block one expert is named by exactly 24 rows. `cache_lengths`: in every aligned block of 128 rows of one micro-batch some row has length 16.
All inputs are finite; a program needn't handle non-finite values.
Results may differ from the reference program's by a relative error of at most 0.0058.
Values may be sent and summed in bfloat16 or wider, within the bound.
A program may use at most 128 MiB of HBM per device.

```python
import math
import jax
import jax.numpy as jnp
import numpy as np
from jax import lax

D = 3584
HEADS = 32
HD = 128
EXPERTS = 32
TOPK = 3
FF_E = 2560
FF_S = 2560
RM = 128
L = 16
MB = 2
ROWS_MB = 1024
CAP = 24
N_ROLE = 2
N_GRP = 8
N_TP = 16


def draw_queries(key, part):
    key = jax.random.fold_in(key, 12)
    base = jnp.clip(jax.random.normal(key, (MB, ROWS_MB, HEADS, HD), jnp.float32), -6.0, 6.0)
    return base.reshape(MB, ROWS_MB, HEADS * HD).astype(jnp.bfloat16)


def draw_kv_cache(key, part):
    key = jax.random.fold_in(key, 11)
    first, second = jax.random.split(key)
    cache_keys = jnp.clip(jax.random.normal(first, (MB, ROWS_MB, L, HD), jnp.float32), -6.0, 6.0)
    cache_values = jnp.clip(jax.random.normal(second, (MB, ROWS_MB, L, HD), jnp.float32), -6.0, 6.0)
    return jnp.concatenate([cache_keys, cache_values], axis=-1).astype(jnp.bfloat16)


def draw_residual(key, part):
    key = jax.random.fold_in(key, 13)
    first, second, third = jax.random.split(key, 3)
    column_scale = jnp.exp(jax.random.uniform(second, (D,), jnp.float32, 0.0, math.log(10.0)))
    row_scale = jnp.exp(jax.random.uniform(third, (MB, ROWS_MB, 1), jnp.float32, 0.0, math.log(10.0)))
    positions = jnp.arange(D).astype(jnp.float32) / D
    entries = jnp.clip(jax.random.normal(first, (MB, ROWS_MB, D), jnp.float32), -6.0, 6.0)
    rise = jnp.exp(positions * math.log(3.0))
    return (entries * row_scale * column_scale * rise * 0.05).astype(jnp.bfloat16)


def draw_cache_lengths(key, part):
    key = jax.random.fold_in(key, 14)
    first, second = jax.random.split(key)
    block_count = ROWS_MB // RM
    lengths = jax.random.randint(first, (MB, block_count, RM), 2, L + 1)
    longest = jax.random.randint(second, (MB, block_count, 1), 0, RM)
    inside = jnp.arange(RM)[None, None, :]
    lengths = jnp.where(inside == longest, L, lengths)
    return lengths.reshape(MB, ROWS_MB).astype(jnp.int32)


def raised(result, key, source, target, shards_of, factor):
    def block_of(dim):
        return (jnp.arange(result.shape[dim]) // (result.shape[dim] // shards_of)).reshape((-1,) + (1,) * (result.ndim - 1 - dim))

    one_side = jax.random.permutation(key, shards_of)[block_of(target)]
    far = (block_of(target) + shards_of // 2) % shards_of
    return jnp.where((block_of(source) == one_side) | (block_of(source) == far), factor * result, result)


def level_of(rng, dims, cuts, smallest, top_value):
    level = 1.0
    for position, blocks in cuts:
        draws = jax.random.uniform(jax.random.fold_in(jax.random.fold_in(rng, 6), position), (blocks,), jnp.float32, smallest / len(cuts), top_value / len(cuts))
        level = level * jnp.repeat(jnp.exp(draws), dims[position] // blocks).reshape((-1,) + (1,) * (len(dims) - 1 - position))
    return level


def routed_block(own_key, own, number, rows, number_of, top, most, slope):
    sequence = jax.random.permutation(own_key, number_of)
    packed, usual = shares(number_of, rows * top, most, slope, True), shares(number_of, rows * top, most, slope, False)
    places = jnp.arange(number_of)

    def named(sizes, rotation):
        used = int((sizes > 0).sum())
        fixed = max(1, used // 4)
        shifted = fixed + (places - fixed + rotation * (used - fixed)) % max(1, number_of - fixed)
        return jnp.zeros((number_of,), jnp.int32).at[sequence[jnp.where(places < fixed, places, shifted)]].set(jnp.asarray(sizes, jnp.int32))

    sizes = jnp.where(number % 4 == 0, named(packed, number // 4), named(usual, number - number // 4 - 1))
    mixed = jax.random.permutation(jax.random.fold_in(own, 3), number_of)
    donor, sink = mixed[0:number_of // 2 * 2:2], mixed[1:number_of // 2 * 2:2]
    margin = jnp.minimum(sizes[donor] - 1, most - sizes[sink]) // 2
    margin = jnp.where((donor == sequence[0]) | (sink == sequence[0]) | (sizes[sink] == 0), 0, jnp.maximum(margin, 0))
    shifted = jax.random.randint(jax.random.fold_in(own, 4), (number_of // 2,), 0, 1 << 20) % (margin + 1)
    sizes = sizes.at[donor].add(-shifted).at[sink].add(shifted)
    labels = jnp.searchsorted(jnp.cumsum(sizes), jnp.arange(rows * top), side="right").astype(jnp.int32)
    table = labels.reshape(top, rows).T
    table = table[jax.random.permutation(jax.random.fold_in(own, 1), rows)]
    rotation = jax.random.randint(jax.random.fold_in(own, 2), (rows, 1), 0, top)
    return jnp.take_along_axis(table, (jnp.arange(top)[None, :] + rotation) % top, axis=1)


def shares(count, total, most, slope, full):
    loads = [(1 << 20) // math.isqrt(rank ** slope) + 1 for rank in range(1, count + 1)]
    largest = most if full else min(most, max(-(-total // count), total * loads[0] // sum(loads)))
    least = 1 if total - largest >= count - 1 else 0
    given, rest = [largest] + [least] * (count - 1), total - largest - least * (count - 1)
    while rest > 0:
        movable = [i for i in range(1, count) if given[i] < largest] or [i for i in range(1, count) if given[i] < most]
        pool, remaining = sum([loads[i] for i in movable]), rest
        for i in movable:
            addition = min(most - given[i], max(1, remaining * loads[i] // pool), rest)
            given[i] = given[i] + addition
            rest = rest - addition
    return np.array(given)


def noise(rng, dims, width, bound, shards=(), kind=jnp.bfloat16):
    loudness = level_of(rng, dims, shards, -0.22, 0.18) if shards else 1.0
    values = jax.random.normal(rng, dims, jnp.float32) * width * loudness
    return jnp.minimum(jnp.maximum(values, -bound), bound).astype(kind)


def heavy_noise(stream_key, dims, deviation, most, pieces, heavy, kind=jnp.bfloat16):
    drawn = deviation * jax.random.normal(stream_key, dims, jnp.float32)
    if pieces:
        drawn = drawn * level_of(stream_key, dims, pieces, -0.22, 0.18)
    return jnp.clip(raised(drawn, jax.random.fold_in(stream_key, 3), *heavy), -most, most).astype(kind)


def setup_inputs(seed: int = 0) -> dict:
    key_of = jax.random.split(jax.random.key(seed), 13)
    residual = draw_residual(jax.random.fold_in(key_of[12], 71), 0)
    queries = draw_queries(jax.random.fold_in(key_of[12], 71), 0)
    kv_cache = draw_kv_cache(jax.random.fold_in(key_of[12], 71), 0)
    cache_lengths = draw_cache_lengths(jax.random.fold_in(key_of[12], 71), 0)
    out_proj = heavy_noise(key_of[4], (HEADS * HD, D), (HEADS * HD) ** -0.5, 0.125, ((0, 16),), (0, 1, 16, 2.0))
    norm_gain = jnp.clip(1.0 + 0.18 * jax.random.normal(key_of[5], (D,), jnp.float32), 0.099609375, 1.8984375).astype(jnp.bfloat16)
    routes_keys = jax.random.split(jax.random.fold_in(key_of[6], 1), MB * ROWS_MB // RM)
    routes_turns = jax.random.permutation(jax.random.fold_in(key_of[6], 3), MB * ROWS_MB // RM)
    routes = jax.vmap(lambda own, number: routed_block(jax.random.fold_in(key_of[6], 2), own, number, RM, EXPERTS, TOPK, CAP, 2))(routes_keys, routes_turns).reshape((MB, ROWS_MB, TOPK))
    gate_weights = jnp.clip(0.2 + 0.8 * jax.random.uniform(key_of[7], (MB, ROWS_MB, TOPK), jnp.float32) ** level_of(key_of[7], (MB, ROWS_MB, TOPK), ((0, 2), (1, 8)), -0.2, 0.2), 0.2, 1.0)
    expert_in = noise(key_of[8], (EXPERTS, 2, FF_E, D), D ** -0.5, 0.09375, ((0, 16), (2, 16)))
    expert_out = heavy_noise(key_of[9], (EXPERTS, FF_E, D), FF_E ** -0.5, 0.15625, ((0, 16), (1, 16)), (1, 2, 16, 2.0))
    shared_in = noise(key_of[10], (2, FF_S, D), D ** -0.5, 0.09375, ((1, 16),))
    shared_out = heavy_noise(key_of[11], (FF_S, D), FF_S ** -0.5, 0.15625, ((0, 16),), (0, 1, 16, 2.0))
    return {"residual": residual, "queries": queries, "kv_cache": kv_cache, "cache_lengths": cache_lengths, "out_proj": out_proj, "norm_gain": norm_gain, "routes": routes, "gate_weights": gate_weights, "expert_in": expert_in, "expert_out": expert_out, "shared_in": shared_in, "shared_out": shared_out}


def rms_scale(hidden, norm_gain):
    values = hidden.astype(jnp.float32)
    mean_square = lax.optimization_barrier(jnp.mean(values * values, axis=-1, keepdims=True))
    scaled = values * lax.rsqrt(mean_square + 1e-06) * norm_gain.astype(jnp.float32)
    return scaled.astype(jnp.bfloat16)

def reference(residual, queries, kv_cache, cache_lengths, out_proj, norm_gain, routes, gate_weights, expert_in, expert_out, shared_in, shared_out):
    total_rows = MB * ROWS_MB
    query_heads = queries.reshape(total_rows, HEADS, HD).astype(jnp.float32)
    cache_rows = kv_cache.reshape(total_rows, L, 2 * HD)
    cache_keys = cache_rows[:, :, :HD].astype(jnp.float32)
    cache_values = cache_rows[:, :, HD:].astype(jnp.float32)
    scores = jnp.einsum('rhd,rld->rhl', query_heads, cache_keys) * HD ** (-0.5)
    visible = jnp.arange(L, dtype=jnp.int32)[None, None, :] < cache_lengths.reshape(total_rows)[:, None, None]
    scores = jnp.where(visible, scores, -1e+30)
    maximum = lax.optimization_barrier(jnp.max(scores, axis=-1, keepdims=True))
    exponent = jnp.where(visible, jnp.exp(scores - maximum), 0.0)
    attn_weights = (exponent / lax.optimization_barrier(jnp.sum(exponent, axis=-1, keepdims=True))).astype(jnp.bfloat16)
    context = jnp.einsum('rhl,rld->rhd', attn_weights.astype(jnp.float32), cache_values).astype(jnp.bfloat16)
    attended = jnp.dot(context.reshape(total_rows, HEADS * HD), out_proj, preferred_element_type=jnp.float32)
    hidden = (residual.reshape(total_rows, D).astype(jnp.float32) + attended).astype(jnp.bfloat16)
    normed = rms_scale(hidden, norm_gain)
    shared_gate = jnp.dot(normed, shared_in[0].T, preferred_element_type=jnp.float32)
    shared_up = jnp.dot(normed, shared_in[1].T, preferred_element_type=jnp.float32)
    shared_act = (jax.nn.silu(shared_gate) * shared_up).astype(jnp.bfloat16)
    shared_branch = jnp.dot(shared_act, shared_out, preferred_element_type=jnp.float32)
    flat_routes = routes.reshape(total_rows, TOPK)
    flat_gates = gate_weights.reshape(total_rows, TOPK)
    row_ids = jnp.arange(total_rows, dtype=jnp.int32)
    limit = N_ROLE * N_GRP * CAP

    def add_expert(carry, expert):
        chosen = flat_routes == expert
        weight = lax.optimization_barrier(jnp.sum(jnp.where(chosen, flat_gates, 0.0), axis=1))
        is_routed = jnp.any(chosen, axis=1)
        sort_keys = jnp.where(is_routed, row_ids, row_ids + total_rows).astype(jnp.int32)
        row_order = jnp.argsort(sort_keys, stable=True)[:limit].astype(jnp.int32)
        picked = normed[row_order]
        gate_pre = jnp.dot(picked, expert_in[expert, 0].T, preferred_element_type=jnp.float32)
        up_pre = jnp.dot(picked, expert_in[expert, 1].T, preferred_element_type=jnp.float32)
        expert_act = (jax.nn.silu(gate_pre) * up_pre).astype(jnp.bfloat16)
        blocks = expert_act.reshape(limit, N_TP, FF_E // N_TP).astype(jnp.float32)
        down_blocks = expert_out[expert].reshape(N_TP, FF_E // N_TP, D).astype(jnp.float32)
        partial_value = jnp.einsum('rtf,tfd->rtd', blocks, down_blocks).astype(jnp.bfloat16)
        partial_value = lax.optimization_barrier(partial_value)
        expert_result = lax.optimization_barrier(jnp.sum(partial_value.astype(jnp.float32), axis=1))
        contribution = expert_result * weight[row_order][:, None]
        return (carry.at[row_order].add(contribution), None)
    routed, _ = lax.scan(add_expert, jnp.zeros((total_rows, D), jnp.float32), jnp.arange(EXPERTS, dtype=jnp.int32))
    layer_out = (hidden.astype(jnp.float32) + shared_branch + routed).astype(jnp.bfloat16)
    return layer_out.reshape(MB, ROWS_MB, D)
```

```python
import functools

import jax
import jax.numpy as jnp
from jax import lax
from jax.experimental import pallas as pl
from jax.experimental.pallas import tpu as pltpu
from jax.sharding import PartitionSpec as P

HD = 128
EXPERTS = 32
TOPK = 3
L = 16
CAP = 24
UNIT = 2 * CAP
MESH = pl.DeviceIdType.MESH
BF16 = jnp.bfloat16
F32 = jnp.float32
VMEM_LIMIT = 50 * 1024 * 1024


def places():
    role, grp, tp = lax.axis_index("role"), lax.axis_index("grp"), lax.axis_index("tp")
    return role, grp // 4, grp % 4, tp // 4, tp % 4


def flip(a, b):
    return (a + b) % 2


def xor4(a, b):
    return 2 * flip(a // 2, b // 2) + flip(a % 2, b % 2)


def z_mates(z):
    return {1: xor4(z, 1), 2: (z + 2) % 4, 3: 3 - z}


def device(role, zh, y, z, x):
    return {"role": role, "grp": zh * 4 + y, "tp": z * 4 + x}


def partners(role, zh, y, z, x):
    there = (flip(role, x % 2), 1 - zh)
    return device(*there, xor4(y, z), 3 - z, x), device(*there, xor4(y, 3 - z), 3 - z, x)


def meet(devices):
    barrier = pltpu.get_barrier_semaphore()
    for one in devices:
        pl.semaphore_signal(barrier, inc=1, device_id=one, device_id_type=MESH)
    pl.semaphore_wait(barrier, len(devices))


def plane_mates(role, zh, y, z, x):
    mates = [device(role, zh, y, z, (x + 1) % 4), device(role, zh, y, z, (x + 3) % 4)]
    return mates + [device(role, zh, y, one, x) for one in z_mates(z).values()]


def column_mates(role, zh, y, z, x):
    mates = [device(one, zh, (y + step) % 4, z, x) for step in (1, 3) for one in (0, 1)]
    return mates + [device(1 - role, zh, y, z, x)]


def send(src, dst, send_sem, recv_sem, to):
    copy = pltpu.make_async_remote_copy(
        src_ref=src, dst_ref=dst, send_sem=send_sem, recv_sem=recv_sem, device_id=to, device_id_type=MESH
    )
    copy.start()
    return copy


class PlaneSum:
    def __init__(self, here, part, half, rx1, tx, rx2, zt, zrx, s1, r1, s2, r2, zs, zr):
        self.here, self.part, self.half = here, part, half
        self.rx1, self.tx, self.rx2, self.zt, self.zrx = rx1, tx, rx2, zt, zrx
        self.s1, self.r1, self.s2, self.r2, self.zs, self.zr = s1, r1, s2, r2, zs, zr
        role, zh, y, z, x = here
        mates = z_mates(z)
        self.order = [mates[2], mates[3], mates[1], z]
        self.right, self.left = (x + 1) % 4, (x + 3) % 4
        self.to_right = device(role, zh, y, z, self.right)
        self.to_left = device(role, zh, y, z, self.left)
        self.copies = []
        self.first, self.second, self.zcopies = {}, {}, []

    def begin(self, i):
        x = self.here[4]
        far = (x + 2) % 4
        base = self.order[i] * 4
        for d, (to, near) in enumerate(((self.to_right, self.right), (self.to_left, self.left))):
            self.first[i, d] = send(
                self.half(self.part, base + far, d), self.rx1.at[i, d], self.s1.at[i, d], self.r1.at[i, d], to
            )
            self.second[i, d, 1 - d] = send(
                self.half(self.part, base + near, 1 - d),
                self.rx2.at[i, d, 1 - d],
                self.s2.at[i, d, 1 - d],
                self.r2.at[i, d, 1 - d],
                to,
            )

    def middle(self, i):
        base = self.order[i] * 4
        for d, (to, near) in enumerate(((self.to_right, self.right), (self.to_left, self.left))):
            self.first[i, d].wait_recv()
            own = self.half(self.part, base + near, d)[...]
            self.tx[i, d] = (self.rx1[i, d].astype(F32) + own.astype(F32)).astype(BF16)
            self.second[i, d, d] = send(
                self.tx.at[i, d], self.rx2.at[i, d, d], self.s2.at[i, d, d], self.r2.at[i, d, d], to
            )

    def line(self, i, h):
        x = self.here[4]
        own = self.half(self.part, self.order[i] * 4 + x, h)[...].astype(F32)
        return own + self.rx2[i, 0, h].astype(F32) + self.rx2[i, 1, h].astype(F32)

    def end(self, i):
        role, zh, y, z, x = self.here
        for d in range(2):
            for h in range(2):
                self.second[i, d, h].wait_recv()
        if i == 3:
            return
        for h in range(2):
            self.zt[i, h] = self.line(i, h).astype(BF16)
            self.zcopies.append(
                send(
                    self.zt.at[i, h],
                    self.zrx.at[i, h],
                    self.zs.at[i, h],
                    self.zr.at[i, h],
                    device(role, zh, y, self.order[i], x),
                )
            )

    def total(self, h):
        for i in range(3):
            self.zcopies[2 * i + h].wait_recv()
        value = self.line(3, h)
        for i in range(3):
            value = value + self.zrx[i, h].astype(F32)
        return value

    def drain(self):
        for copy in list(self.first.values()) + list(self.second.values()) + self.zcopies:
            copy.wait_send()

    def whole(self, between=lambda: None):
        for i in range(4):
            self.begin(i)
        self.middle(0)
        self.middle(1)
        between()
        self.end(0)
        self.middle(2)
        self.end(1)
        self.middle(3)
        self.end(2)
        self.end(3)


def plane_sum_scratch(half):
    dma = pltpu.SemaphoreType.DMA
    return [
        pltpu.VMEM((4, 2) + half, BF16),
        pltpu.VMEM((4, 2) + half, BF16),
        pltpu.VMEM((4, 2, 2) + half, BF16),
        pltpu.VMEM((3, 2) + half, BF16),
        pltpu.VMEM((3, 2) + half, BF16),
        dma((4, 2)),
        dma((4, 2)),
        dma((4, 2, 2)),
        dma((4, 2, 2)),
        dma((3, 2)),
        dma((3, 2)),
    ]


class PlaneGather:
    def __init__(self, here, out, half, zs, zr, xs, xr, fs, fr):
        self.here, self.out, self.half = here, out, half
        self.zs, self.zr, self.xs, self.xr, self.fs, self.fr = zs, zr, xs, xr, fs, fr
        role, zh, y, z, x = here
        mates = z_mates(z)
        self.order = [z, mates[1], mates[2], mates[3]]
        self.to_right = device(role, zh, y, z, (x + 1) % 4)
        self.to_left = device(role, zh, y, z, (x + 3) % 4)
        self.zcopies, self.near, self.far = {}, {}, {}

    def begin(self):
        role, zh, y, z, x = self.here
        mine = z * 4 + x
        self.start(0)
        for m in (3, 2, 1):
            for h in range(2):
                block = self.half(self.out, mine, h)
                self.zcopies[m, h] = send(
                    block, block, self.zs.at[m - 1, h], self.zr.at[m - 1, h], device(role, zh, y, self.order[m], x)
                )

    def start(self, i):
        x = self.here[4]
        slot = self.order[i] * 4 + x
        if i > 0:
            for h in range(2):
                self.zcopies[i, h].wait_recv()
        for h in range(2):
            for d, to in enumerate((self.to_right, self.to_left)):
                block = self.half(self.out, slot, h if d == 0 else 1 - h)
                k = h if d == 0 else 1 - h
                self.near[i, d, k] = send(block, block, self.xs.at[i, d, k], self.xr.at[i, d, k], to)

    def pass_on(self, i):
        x = self.here[4]
        base = self.order[i] * 4
        for d, (to, slot) in enumerate(((self.to_right, (x + 3) % 4), (self.to_left, (x + 1) % 4))):
            self.near[i, d, d].wait_recv()
            block = self.half(self.out, base + slot, d)
            self.far[i, d] = send(block, block, self.fs.at[i, d], self.fr.at[i, d], to)

    def finish(self):
        for (i, d, k), copy in self.near.items():
            if k != d:
                copy.wait_recv()
        for copy in self.far.values():
            copy.wait_recv()
        for copies in (self.zcopies, self.near, self.far):
            for copy in copies.values():
                copy.wait_send()

    def whole(self, between=lambda: None):
        self.begin()
        self.pass_on(0)
        self.start(1)
        between()
        self.start(2)
        self.pass_on(1)
        self.start(3)
        self.pass_on(2)
        self.pass_on(3)
        self.finish()


def plane_gather_scratch():
    dma = pltpu.SemaphoreType.DMA
    return [dma((3, 2)), dma((3, 2)), dma((4, 2, 2)), dma((4, 2, 2)), dma((4, 2)), dma((4, 2))]


class ColumnSwap:
    def __init__(self, here, src, dst, relay, s_near, r_near, s_rel, r_rel, s_fwd, r_fwd, s_own, r_own):
        self.here, self.src, self.dst, self.relay = here, src, dst, relay
        self.sems = (s_near, r_near, s_rel, r_rel, s_fwd, r_fwd, s_own, r_own)
        self.rel, self.fwd, self.near = {}, {}, {}

    def begin(self):
        role, zh, y, z, x = self.here
        s_near, r_near, s_rel, r_rel, s_fwd, r_fwd, s_own, r_own = self.sems
        width = self.src.shape[3] // 2
        for q in range(2):
            for d, step in enumerate((1, 3)):
                self.rel[d, q] = send(
                    self.src.at[q, (y + 2) % 4, :, pl.ds(d * width, width)],
                    self.relay.at[d, q],
                    s_rel.at[d, q],
                    r_rel.at[d, q],
                    device(role, zh, (y + step) % 4, z, x),
                )
        for q in range(2):
            for d, step in enumerate((1, 3)):
                other = (y + step) % 4
                self.near[d, q] = send(
                    self.src.at[q, other],
                    self.dst.at[role, y],
                    s_near.at[d, q],
                    r_near.at[d, role],
                    device(q, zh, other, z, x),
                )
        self.core = send(
            self.src.at[1 - role, y], self.dst.at[role, y], s_own.at[0], r_own.at[0], device(1 - role, zh, y, z, x)
        )
        self.own = pltpu.make_async_copy(self.src.at[role, y], self.dst.at[role, y], s_own.at[1])
        self.own.start()

    def pass_on(self):
        role, zh, y, z, x = self.here
        s_near, r_near, s_rel, r_rel, s_fwd, r_fwd, s_own, r_own = self.sems
        width = self.src.shape[3] // 2
        for q in range(2):
            for d, step in enumerate((1, 3)):
                self.rel[d, q].wait_recv()
                origin = (y + 4 - step) % 4
                self.fwd[d, q] = send(
                    self.relay.at[d, q],
                    self.dst.at[role, origin, :, pl.ds(d * width, width)],
                    s_fwd.at[d, q],
                    r_fwd.at[d, role],
                    device(q, zh, (y + step) % 4, z, x),
                )

    def finish(self):
        role, zh, y, z, x = self.here
        s_near, r_near, s_rel, r_rel, s_fwd, r_fwd, s_own, r_own = self.sems
        width = self.src.shape[3] // 2
        for q in range(2):
            for d, step in enumerate((1, 3)):
                block = self.dst.at[q, (y + 4 - step) % 4]
                pltpu.make_async_copy(block, block, r_near.at[d, q]).wait()
                block = self.dst.at[q, (y + 2) % 4, :, pl.ds(d * width, width)]
                pltpu.make_async_copy(block, block, r_fwd.at[d, q]).wait()
        self.core.wait_recv()
        self.own.wait()
        for copies in (self.rel, self.fwd, self.near):
            for copy in copies.values():
                copy.wait_send()
        self.core.wait_send()


def column_scratch(rows, width):
    dma = pltpu.SemaphoreType.DMA
    return [pltpu.VMEM((2, 2, rows, width // 2), BF16)] + [dma((2, 2))] * 6 + [dma((2,))] * 2


def row_half(ref, slot, h):
    rows = ref.shape[1] // 2
    return ref.at[slot, pl.ds(h * rows, rows), :]


def lane_half(ref, slot, h):
    width = ref.shape[2] // 2
    return ref.at[slot, :, pl.ds(h * width, width)]


def hidden_kernel(part, resid, out, *scratch):
    here = places()
    meet(plane_mates(*here))
    mine = here[3] * 4 + here[4]
    sums = PlaneSum(here, part, row_half, *scratch[:11])
    sums.whole()
    rows = resid.shape[0] // 2
    for h in range(2):
        value = sums.total(h) + resid[pl.ds(h * rows, rows), :].astype(F32)
        out[mine, pl.ds(h * rows, rows), :] = value.astype(BF16)
    PlaneGather(here, out, row_half, *scratch[11:]).whole()
    sums.drain()


def output_kernel(part, hidden, out, *scratch):
    here = places()
    meet(plane_mates(*here))
    sums = PlaneSum(here, part, row_half, *scratch)
    sums.whole()
    rows = hidden.shape[0] // 2
    for h in range(2):
        value = sums.total(h) + hidden[pl.ds(h * rows, rows), :].astype(F32)
        out[pl.ds(h * rows, rows), :] = value.astype(BF16)
    sums.drain()


def dispatch_kernel(same, cross, got_same, got_cross, swap_s, swap_r, *scratch):
    here = places()
    role, zh, y, z, x = here
    to, source = partners(*here)
    meet(plane_mates(*here) + column_mates(*here) + [to, source])
    swap = send(cross, got_cross.at[(3 - z) * 4 + x], swap_s.at[0], swap_r.at[0], to)
    column = ColumnSwap(here, same, got_same, *scratch[:9])
    column.begin()
    swap.wait_recv()
    gather = PlaneGather(here, got_cross, lane_half, *scratch[9:])
    gather.whole(between=column.pass_on)
    column.finish()
    swap.wait_send()


def return_kernel(same, cross, got_same, got_cross, done, swap_s, swap_r, *scratch):
    here = places()
    to, source = partners(*here)
    meet(plane_mates(*here) + column_mates(*here) + [to, source])
    column = ColumnSwap(here, same, got_same, *scratch[:9])
    sums = PlaneSum(here, cross, lane_half, *scratch[9:])
    for i in range(1):
        sums.begin(i)
    column.begin()
    for i in range(1, 4):
        sums.begin(i)
    sums.middle(0)
    sums.middle(1)
    column.pass_on()
    sums.end(0)
    sums.middle(2)
    sums.end(1)
    sums.middle(3)
    sums.end(2)
    sums.end(3)
    width = done.shape[1] // 2
    for h in range(2):
        done[:, pl.ds(h * width, width)] = sums.total(h).astype(BF16)
    swap = send(done, got_cross, swap_s.at[0], swap_r.at[0], source)
    column.finish()
    sums.drain()
    swap.wait()


def call(kernel, collective_id, out_shape, scratch, *operands):
    vmem = pl.BlockSpec(memory_space=pltpu.VMEM)
    many = isinstance(out_shape, (list, tuple))
    return pl.pallas_call(
        kernel,
        out_shape=out_shape,
        in_specs=[vmem] * len(operands),
        out_specs=[vmem] * len(out_shape) if many else vmem,
        scratch_shapes=scratch,
        compiler_params=pltpu.CompilerParams(
            collective_id=collective_id, has_side_effects=True, vmem_limit_bytes=VMEM_LIMIT
        ),
    )(*operands)


def shape(*dims):
    return jax.ShapeDtypeStruct(dims, BF16)


def slot_places(routes_local):
    rows = routes_local.shape[0]
    ids = jnp.arange(EXPERTS, dtype=jnp.int32)
    named = routes_local[:, :, None] == ids[None, None, :]
    chosen = jnp.any(named, axis=1).astype(BF16)
    order = jnp.arange(rows, dtype=jnp.int32)
    earlier = (order[:, None] > order[None, :]).astype(BF16)
    before = jnp.dot(earlier, chosen, preferred_element_type=F32)
    position = jnp.sum(jnp.where(named, before[:, None, :], 0.0), axis=2).astype(jnp.int32)
    return routes_local * CAP + position


def body(
    residual,
    queries,
    kv_cache,
    cache_lengths,
    out_proj,
    norm_gain,
    routes,
    gate_weights,
    expert_in,
    expert_out,
    shared_in,
    shared_out,
):
    rows = residual.shape[1]
    part = residual.shape[2]
    tp_count = lax.axis_size("tp")
    width = part * tp_count
    half_width = width // 2
    role, zh, y, z, x = places()
    head_count = queries.shape[2] // HD

    query_heads = queries.reshape(rows, head_count, HD)
    cache_rows = kv_cache.reshape(rows, L, 2 * HD)
    cache_keys = cache_rows[:, :, :HD]
    cache_values = cache_rows[:, :, HD:]
    scores = jnp.einsum("rhd,rld->rhl", query_heads, cache_keys, preferred_element_type=F32) * HD ** (-0.5)
    visible = jnp.arange(L, dtype=jnp.int32)[None, None, :] < cache_lengths.reshape(rows)[:, None, None]
    scores = jnp.where(visible, scores, -1e30)
    maximum = jnp.max(scores, axis=-1, keepdims=True)
    exponent = jnp.where(visible, jnp.exp(scores - maximum), 0.0)
    attn_weights = (exponent / jnp.sum(exponent, axis=-1, keepdims=True)).astype(BF16)
    context = jnp.einsum("rhl,rld->rhd", attn_weights, cache_values, preferred_element_type=F32).astype(BF16)
    context = context.reshape(rows, head_count * HD)
    attended = jnp.einsum("kd,rk->dr", out_proj, context, preferred_element_type=F32).astype(BF16)

    small_half = (part // 2, rows)
    hidden = call(
        hidden_kernel,
        1,
        shape(tp_count, part, rows),
        plane_sum_scratch(small_half) + plane_gather_scratch(),
        attended.reshape(tp_count, part, rows),
        residual.reshape(rows, part).T,
    )
    hidden_part = lax.dynamic_index_in_dim(hidden, z * 4 + x, 0, keepdims=False)
    hidden_wide = hidden.reshape(width, rows).astype(F32)
    mean_square = jnp.mean(hidden_wide * hidden_wide, axis=0, keepdims=True)
    normed = (hidden_wide * lax.rsqrt(mean_square + 1e-06) * norm_gain.astype(F32)[:, None]).astype(BF16)

    slot_index = slot_places(routes.reshape(rows, TOPK))
    gates = gate_weights.reshape(rows, TOPK)
    owners = jnp.arange(2, dtype=jnp.int32)[:, None] * 8 + zh * 4 + jnp.arange(4, dtype=jnp.int32)[None, :]
    inside = jnp.arange(UNIT, dtype=jnp.int32)
    same_ids = (owners.reshape(8)[:, None] * UNIT + inside[None, :]).reshape(8 * UNIT)
    cross_owner = flip(role, x % 2) * 8 + (1 - zh) * 4 + xor4(y, z)
    cross_ids = cross_owner * UNIT + inside
    cross_half = x // 2

    same_hit = same_ids[:, None, None] == slot_index[None, :, :]
    cross_hit = cross_ids[:, None, None] == slot_index[None, :, :]
    same_pick = jnp.any(same_hit, axis=2).astype(BF16)
    cross_pick = jnp.any(cross_hit, axis=2).astype(BF16)
    same_rows = jnp.einsum("sr,dr->sd", same_pick, normed, preferred_element_type=F32).astype(BF16)
    normed_half = lax.dynamic_slice_in_dim(normed, cross_half * half_width, half_width, 0)
    cross_rows = jnp.einsum("sr,dr->sd", cross_pick, normed_half, preferred_element_type=F32).astype(BF16)

    dma = pltpu.SemaphoreType.DMA
    got_same, got_cross = call(
        dispatch_kernel,
        2,
        [shape(2, 4, UNIT, width), shape(tp_count, UNIT, half_width)],
        [dma((1,)), dma((1,))] + column_scratch(UNIT, width) + plane_gather_scratch(),
        same_rows.reshape(2, 4, UNIT, width),
        cross_rows,
    )

    shared_pre = jnp.einsum("dr,gfd->rgf", normed, shared_in, preferred_element_type=F32)
    shared_act = (jax.nn.silu(shared_pre[:, 0]) * shared_pre[:, 1]).astype(BF16)
    shared_partial = jnp.einsum("fd,rf->dr", shared_out, shared_act, preferred_element_type=F32)

    hidden_units = expert_out.shape[1]
    w_in = expert_in.reshape(4 * hidden_units, width)
    w_out = expert_out.reshape(2 * hidden_units, width)

    def activate(pre):
        pre = pre.reshape(-1, 2, 2, hidden_units)
        act = jax.nn.silu(pre[:, :, 0]) * pre[:, :, 1]
        slot_expert = (jnp.arange(act.shape[0], dtype=jnp.int32) % UNIT) // CAP
        act = jnp.where(slot_expert[:, None, None] == jnp.arange(2, dtype=jnp.int32)[None, :, None], act, 0.0)
        return act.reshape(-1, 2 * hidden_units).astype(BF16)

    same_pre = jnp.einsum("sd,fd->sf", got_same.reshape(8 * UNIT, width), w_in, preferred_element_type=F32)
    cross_in = got_cross.reshape(4, 2, 2 * UNIT, half_width)
    cross_pre = sum(
        jnp.einsum(
            "sd,fd->sf",
            cross_in[:, h].reshape(8 * UNIT, half_width),
            w_in[:, h * half_width : (h + 1) * half_width],
            preferred_element_type=F32,
        )
        for h in range(2)
    )
    same_out = jnp.dot(activate(same_pre), w_out, preferred_element_type=F32).astype(BF16)
    cross_act = activate(cross_pre)
    cross_out = jnp.stack(
        [
            jnp.dot(cross_act, w_out[:, h * half_width : (h + 1) * half_width], preferred_element_type=F32)
            .astype(BF16)
            .reshape(4, 2 * UNIT, half_width)
            for h in range(2)
        ],
        axis=1,
    )

    back_same, back_cross, _ = call(
        return_kernel,
        3,
        [shape(2, 4, UNIT, width), shape(UNIT, half_width), shape(UNIT, half_width)],
        [dma((1,)), dma((1,))] + column_scratch(UNIT, width) + plane_sum_scratch((UNIT, half_width // 2)),
        same_out.reshape(2, 4, UNIT, width),
        cross_out.reshape(tp_count, UNIT, half_width),
    )

    def weigh(hit, table):
        weight = jnp.sum(jnp.where(hit, gates[None, :, :], 0.0), axis=2)
        high = weight.astype(BF16)
        low = (weight - high.astype(F32)).astype(BF16)
        return jnp.einsum("sd,sr->dr", table, high, preferred_element_type=F32) + jnp.einsum(
            "sd,sr->dr", table, low, preferred_element_type=F32
        )

    routed = weigh(same_hit, back_same.reshape(8 * UNIT, width))
    routed_cross = weigh(cross_hit, back_cross)
    halves = jnp.arange(2, dtype=jnp.int32)[:, None, None]
    branches = (shared_partial + routed).reshape(2, half_width, rows)
    branches = (branches + jnp.where(halves == cross_half, routed_cross[None], 0.0)).astype(BF16)

    layer_out = call(
        output_kernel,
        4,
        shape(part, rows),
        plane_sum_scratch(small_half),
        branches.reshape(tp_count, part, rows),
        hidden_part,
    )
    return layer_out.T.reshape(1, rows, part)


def solution(mesh):
    in_specs = (
        P("role", "grp", "tp"),
        P("role", "grp", "tp"),
        P("role", "grp", None, None),
        P("role", "grp"),
        P("tp", None),
        P(),
        P("role", "grp", None),
        P("role", "grp", None),
        P(("role", "grp"), None, "tp", None),
        P(("role", "grp"), "tp", None),
        P(None, "tp", None),
        P("tp", None),
    )
    out_specs = P("role", "grp", "tp")
    return jax.shard_map(body, mesh=mesh, in_specs=in_specs, out_specs=out_specs, check_vma=False)
```

```python
import functools

import jax
import jax.numpy as jnp
from jax import lax
from jax.experimental import pallas as pl
from jax.experimental.pallas import tpu as pltpu
from jax.sharding import PartitionSpec as P

HD = 128
EXPERTS = 32
TOPK = 3
L = 16
CAP = 24
UNIT = 2 * CAP
MESH = pl.DeviceIdType.MESH
BF16 = jnp.bfloat16
F32 = jnp.float32
VMEM_LIMIT = 50 * 1024 * 1024


def places():
    role, grp, tp = lax.axis_index("role"), lax.axis_index("grp"), lax.axis_index("tp")
    return role, grp // 4, grp % 4, tp // 4, tp % 4


def flip(a, b):
    return (a + b) % 2


def xor4(a, b):
    return 2 * flip(a // 2, b // 2) + flip(a % 2, b % 2)


def z_mates(z):
    return {1: xor4(z, 1), 2: (z + 2) % 4, 3: 3 - z}


def device(role, zh, y, z, x):
    return {"role": role, "grp": zh * 4 + y, "tp": z * 4 + x}


def partners(role, zh, y, z, x):
    there = (flip(role, x % 2), 1 - zh)
    return device(*there, xor4(y, z), 3 - z, x), device(*there, xor4(y, 3 - z), 3 - z, x)


def plane_mates(role, zh, y, z, x):
    mates = [device(role, zh, y, z, (x + 1) % 4), device(role, zh, y, z, (x + 3) % 4)]
    return mates + [device(role, zh, y, one, x) for one in z_mates(z).values()]


def column_mates(role, zh, y, z, x):
    mates = [device(one, zh, (y + step) % 4, z, x) for step in (1, 2, 3) for one in (0, 1)]
    return mates + [device(1 - role, zh, y, z, x)]


def send(src, dst, send_sem, recv_sem, to):
    copy = pltpu.make_async_remote_copy(
        src_ref=src, dst_ref=dst, send_sem=send_sem, recv_sem=recv_sem, device_id=to, device_id_type=MESH
    )
    copy.start()
    return copy


class PlaneSum:
    def __init__(self, here, part, half, rx1, tx, rx2, zt, zrx, s1, r1, s2, r2, zs, zr, own_first=False):
        self.here, self.part, self.half = here, part, half
        self.rx1, self.tx, self.rx2, self.zt, self.zrx = rx1, tx, rx2, zt, zrx
        self.s1, self.r1, self.s2, self.r2, self.zs, self.zr = s1, r1, s2, r2, zs, zr
        role, zh, y, z, x = here
        mates = z_mates(z)
        self.order = [z, mates[1], mates[3], mates[2]] if own_first else [mates[2], mates[3], mates[1], z]
        self.own = 0 if own_first else 3
        self.zslot = {i: n for n, i in enumerate(i for i in range(4) if i != self.own)}
        self.right, self.left = (x + 1) % 4, (x + 3) % 4
        self.to_right = device(role, zh, y, z, self.right)
        self.to_left = device(role, zh, y, z, self.left)
        self.copies = []
        self.first, self.second, self.zcopies = {}, {}, {}

    def begin(self, i):
        x = self.here[4]
        far = (x + 2) % 4
        base = self.order[i] * 4
        for d, (to, near) in enumerate(((self.to_right, self.right), (self.to_left, self.left))):
            self.first[i, d] = send(
                self.half(self.part, base + far, d), self.rx1.at[i, d], self.s1.at[i, d], self.r1.at[i, d], to
            )
            self.second[i, d, 1 - d] = send(
                self.half(self.part, base + near, 1 - d),
                self.rx2.at[i, d, 1 - d],
                self.s2.at[i, d, 1 - d],
                self.r2.at[i, d, 1 - d],
                to,
            )

    def middle(self, i):
        base = self.order[i] * 4
        for d, (to, near) in enumerate(((self.to_right, self.right), (self.to_left, self.left))):
            self.first[i, d].wait_recv()
            own = self.half(self.part, base + near, d)[...]
            self.tx[i, d] = (self.rx1[i, d].astype(F32) + own.astype(F32)).astype(BF16)
            self.second[i, d, d] = send(
                self.tx.at[i, d], self.rx2.at[i, d, d], self.s2.at[i, d, d], self.r2.at[i, d, d], to
            )

    def line(self, i, h):
        x = self.here[4]
        own = self.half(self.part, self.order[i] * 4 + x, h)[...].astype(F32)
        return own + self.rx2[i, 0, h].astype(F32) + self.rx2[i, 1, h].astype(F32)

    def end(self, i):
        role, zh, y, z, x = self.here
        for d in range(2):
            for h in range(2):
                self.second[i, d, h].wait_recv()
        if i == self.own:
            return
        n = self.zslot[i]
        for h in range(2):
            self.zt[n, h] = self.line(i, h).astype(BF16)
            self.zcopies[n, h] = send(
                self.zt.at[n, h],
                self.zrx.at[n, h],
                self.zs.at[n, h],
                self.zr.at[n, h],
                device(role, zh, y, self.order[i], x),
            )

    def total(self, h):
        value = self.line(self.own, h)
        for i in range(3):
            self.zcopies[i, h].wait_recv()
            value = value + self.zrx[i, h].astype(F32)
        return value

    def drain(self):
        for copy in list(self.first.values()) + list(self.second.values()) + list(self.zcopies.values()):
            copy.wait_send()

    def whole(self, between=lambda: None):
        for i in range(4):
            self.begin(i)
        self.middle(0)
        self.middle(1)
        between()
        self.end(0)
        self.middle(2)
        self.end(1)
        self.middle(3)
        self.end(2)
        self.end(3)


def plane_sum_scratch(half):
    dma = pltpu.SemaphoreType.DMA
    return [
        pltpu.VMEM((4, 2) + half, BF16),
        pltpu.VMEM((4, 2) + half, BF16),
        pltpu.VMEM((4, 2, 2) + half, BF16),
        pltpu.VMEM((3, 2) + half, BF16),
        pltpu.VMEM((3, 2) + half, BF16),
        dma((4, 2)),
        dma((4, 2)),
        dma((4, 2, 2)),
        dma((4, 2, 2)),
        dma((3, 2)),
        dma((3, 2)),
    ]


class PlaneGather:
    def __init__(self, here, out, half, zs, zr, xs, xr, fs, fr):
        self.here, self.out, self.half = here, out, half
        self.zs, self.zr, self.xs, self.xr, self.fs, self.fr = zs, zr, xs, xr, fs, fr
        role, zh, y, z, x = here
        mates = z_mates(z)
        self.order = [z, mates[1], mates[3], mates[2]]
        self.to_right = device(role, zh, y, z, (x + 1) % 4)
        self.to_left = device(role, zh, y, z, (x + 3) % 4)
        self.zcopies, self.near, self.far = {}, {}, {}

    def begin(self):
        role, zh, y, z, x = self.here
        mine = z * 4 + x
        self.start(0)
        for m in (1, 2, 3):
            for h in range(2):
                block = self.half(self.out, mine, h)
                self.zcopies[m, h] = send(
                    block, block, self.zs.at[m - 1, h], self.zr.at[m - 1, h], device(role, zh, y, self.order[m], x)
                )

    def start(self, i):
        x = self.here[4]
        slot = self.order[i] * 4 + x
        if i > 0:
            for h in range(2):
                self.zcopies[i, h].wait_recv()
        for h in range(2):
            for d, to in enumerate((self.to_right, self.to_left)):
                block = self.half(self.out, slot, h if d == 0 else 1 - h)
                k = h if d == 0 else 1 - h
                self.near[i, d, k] = send(block, block, self.xs.at[i, d, k], self.xr.at[i, d, k], to)

    def pass_on(self, i):
        x = self.here[4]
        base = self.order[i] * 4
        for d, (to, slot) in enumerate(((self.to_right, (x + 3) % 4), (self.to_left, (x + 1) % 4))):
            self.near[i, d, d].wait_recv()
            block = self.half(self.out, base + slot, d)
            self.far[i, d] = send(block, block, self.fs.at[i, d], self.fr.at[i, d], to)

    def complete(self, i):
        for d in range(2):
            self.near[i, d, 1 - d].wait_recv()
            self.far[i, d].wait_recv()

    def finish(self):
        for copies in (self.zcopies, self.near, self.far):
            for copy in copies.values():
                copy.wait_send()

    def whole(self, between=lambda: None):
        self.begin()
        self.pass_on(0)
        self.start(1)
        between()
        self.start(2)
        self.pass_on(1)
        self.start(3)
        self.pass_on(2)
        self.pass_on(3)
        for i in range(4):
            self.complete(i)
        self.finish()


def plane_gather_scratch():
    dma = pltpu.SemaphoreType.DMA
    return [dma((3, 2)), dma((3, 2)), dma((4, 2, 2)), dma((4, 2, 2)), dma((4, 2)), dma((4, 2))]


def flat_half(ref, slot, h):
    rows = ref.shape[0] // 32
    return ref.at[pl.ds(pl.multiple_of((2 * slot + h) * rows, 16), rows), :]


def lane_half(ref, slot, h):
    width = ref.shape[2] // 2
    return ref.at[slot, :, pl.ds(h * width, width)]


def dot(a, b):
    return jnp.dot(a, b, preferred_element_type=F32)


def dot_rows(a, b):
    return lax.dot_general(a, b, (((1,), (1,)), ((), ())), preferred_element_type=F32)


def split(value):
    high = value.astype(BF16)
    return high, (value - high.astype(F32)).astype(BF16)


def slot_rows(routes):
    count = routes.shape[1]
    ids = lax.broadcasted_iota(jnp.int32, (EXPERTS, count), 0)
    named = [ids == routes[k : k + 1, :] for k in range(TOPK)]
    chosen = jnp.where(named[0] | named[1] | named[2], 1.0, 0.0).astype(BF16)
    earlier = lax.broadcasted_iota(jnp.int32, (count, count), 0) < lax.broadcasted_iota(jnp.int32, (count, count), 1)
    before = dot(chosen, jnp.where(earlier, 1.0, 0.0).astype(BF16))
    place = [jnp.sum(jnp.where(one, before, 0.0), axis=0, keepdims=True).astype(jnp.int32) for one in named]
    return [routes[k : k + 1, :] * CAP + place[k] for k in range(TOPK)]


def unit_hits(slots, owner):
    ids = lax.broadcasted_iota(jnp.int32, (UNIT, slots[0].shape[1]), 0) + owner * UNIT
    return [ids == one for one in slots]


def layer_kernel(names, part, resid, gain, routes, gates, w_in, w_out, s_in, s_out, out, *scratch):
    ref = dict(zip(names, scratch))
    here = places()
    role, zh, y, z, x = here
    mine = z * 4 + x
    rows = routes.shape[1]
    width = gain.shape[1]
    half = width // 2
    units = w_in.shape[2]
    to, source = partners(*here)

    barrier = pltpu.get_barrier_semaphore()
    mates = plane_mates(*here) + column_mates(*here) + [to, source]
    for one in mates:
        pl.semaphore_signal(barrier, inc=1, device_id=one, device_id_type=MESH)

    loads = []
    for j in range(2):
        loads.append((w_in.at[j, 0], ref["gate"].at[pl.ds(j * units, units), :]))
        loads.append((w_in.at[j, 1], ref["up"].at[pl.ds(j * units, units), :]))
        loads.append((w_out.at[j], ref["down"].at[pl.ds(j * units, units), :]))
        loads.append((s_in.at[j], ref["shared_in"].at[j]))
    loads.append((s_out, ref["shared_out"]))
    loads = [pltpu.make_async_copy(a, b, ref["load"].at[i]) for i, (a, b) in enumerate(loads)]
    for one in loads:
        one.start()

    slots = slot_rows(routes[...])
    gate_rows = gates[...]

    def pick(owner):
        hits = unit_hits(slots, owner)
        return jnp.where(hits[0] | hits[1] | hits[2], 1.0, 0.0).astype(BF16)

    def weigh(owner):
        hits = unit_hits(slots, owner)
        return sum(jnp.where(hits[k], gate_rows[k : k + 1, :], 0.0) for k in range(TOPK))

    def owner_of(q, yo):
        return q * 8 + zh * 4 + yo

    cross_owner = flip(role, x % 2) * 8 + (1 - zh) * 4 + xor4(y, z)
    cross_half = x // 2

    pl.semaphore_wait(barrier, len(mates))
    first = PlaneSum(here, part, flat_half, *[ref[f"a{i}"] for i in range(11)])
    first.whole()
    hidden = ref["hidden"]
    step = resid.shape[0] // 2
    for h in range(2):
        value = first.total(h) + resid[pl.ds(h * step, step), :].astype(F32)
        flat_half(hidden, mine, h)[...] = value.astype(BF16)
    PlaneGather(here, hidden, flat_half, *[ref[f"b{i}"] for i in range(6)]).whole()

    normed = ref["normed"]
    tile = 256
    square = jnp.zeros((rows, 1), F32)
    for i in range(width // tile):
        wide = hidden[pl.ds(i * tile, tile), :].astype(F32).T
        square = square + jnp.sum(wide * wide, axis=1, keepdims=True)
        normed[:, pl.ds(i * tile, tile)] = wide.astype(BF16)
    scale = lax.rsqrt(square / width + 1e-06)
    for i in range(width // tile):
        at = pl.ds(i * tile, tile)
        normed[:, at] = (normed[:, at].astype(F32) * scale * gain[:, at]).astype(BF16)

    chosen = pick(cross_owner)
    got_cross = ref["got_cross"]
    swaps = []
    for h in range(2):
        at = pl.ds(h * (half // 2), half // 2)
        from_at = pl.ds(pl.multiple_of(cross_half * half + h * (half // 2), 128), half // 2)
        ref["cross"][:, at] = dot(chosen, normed[:, from_at]).astype(BF16)
        swaps.append(
            send(
                ref["cross"].at[:, at],
                got_cross.at[(3 - z) * 4 + x, :, at],
                ref["swap"].at[0, h],
                ref["swap"].at[1, h],
                to,
            )
        )
    same, got_same, back_same = ref["same"], ref["got_same"], ref["back_same"]
    sent = []

    def pick_into(target, owner):
        chosen = pick(owner)
        for h in range(4):
            at = pl.ds(h * (width // 4), width // 4)
            target[:, at] = dot(chosen, normed[:, at]).astype(BF16)

    for d in (2, 1, 3):
        yo = (y + d) % 4
        for q in range(2):
            pick_into(same.at[q, yo], owner_of(q, yo))
            sent.append(
                send(
                    same.at[q, yo],
                    got_same.at[role, y],
                    ref["near"].at[0, d - 1, q],
                    ref["near"].at[1, d - 1, role],
                    device(q, zh, yo, z, x),
                )
            )
    pick_into(same.at[1 - role, y], owner_of(1 - role, y))
    core = send(
        same.at[1 - role, y], got_same.at[role, y], ref["core"].at[0], ref["core"].at[1], device(1 - role, zh, y, z, x)
    )
    pick_into(got_same.at[role, y], owner_of(role, y))

    for one in loads:
        one.wait()

    for q in range(2):
        for yo in range(4):
            at = pl.ds((q * 4 + yo) * UNIT, UNIT)
            ref["weights"][at, :] = weigh(owner_of(q, yo))
    ref["gate_high"][...], ref["gate_low"][...] = split(ref["weights"][...].T)
    ref["cross_high"][...], ref["cross_low"][...] = split(weigh(cross_owner).T)
    pre = [dot_rows(normed[...], ref["shared_in"][g]) for g in range(2)]
    ref["shared_act"][...] = (jax.nn.silu(pre[0]) * pre[1]).astype(BF16)

    both = 2 * UNIT
    inner = (lax.broadcasted_iota(jnp.int32, (both, 2 * units), 0) % UNIT) >= CAP
    second = lax.broadcasted_iota(jnp.int32, (both, 2 * units), 1) >= units
    own_expert = jnp.logical_not(jnp.logical_xor(inner, second))

    def experts(load, store):
        at = [pl.ds(h * half, half) for h in range(2)]
        found = [load(h) for h in range(2)]
        gate_pre = sum(dot_rows(found[h], ref["gate"][:, at[h]]) for h in range(2))
        up_pre = sum(dot_rows(found[h], ref["up"][:, at[h]]) for h in range(2))
        act = jnp.where(own_expert, jax.nn.silu(gate_pre) * up_pre, 0.0).astype(BF16)
        for h in range(2):
            for c in range(2):
                columns = pl.ds(h * half + c * (half // 2), half // 2)
                result = dot(act, ref["down"][:, columns]).astype(BF16)
                store(h, c, result.reshape(2, UNIT, half // 2))

    made_same, made_cross = ref["made_same"], ref["made_cross"]

    def same_experts(yo):
        def load(h):
            return got_same[:, yo, :, pl.ds(h * half, half)].reshape(both, half)

        def store(h, c, value):
            made_same[:, yo, :, pl.ds(h * half + c * (half // 2), half // 2)] = value

        experts(load, store)

    def cross_experts(zz):
        def load(h):
            return got_cross[pl.ds(zz * 4 + 2 * h, 2)].reshape(both, half)

        def store(h, c, value):
            made_cross[pl.ds(zz * 4 + 2 * h, 2), :, pl.ds(c * (half // 2), half // 2)] = value

        experts(load, store)

    def arrived(block, sem):
        pltpu.make_async_copy(block, block, sem).wait()

    def column_step(d):
        yo = (y + 4 - d) % 4
        for q in range(2):
            arrived(got_same.at[q, yo], ref["near"].at[1, d - 1, q])
        same_experts(yo)
        for q in range(2):
            sent.append(
                send(
                    made_same.at[q, yo],
                    back_same.at[role, y],
                    ref["back"].at[0, d - 1, q],
                    ref["back"].at[1, d - 1, role],
                    device(q, zh, yo, z, x),
                )
            )

    core.wait_recv()
    same_experts(y)
    core_back = send(
        made_same.at[1 - role, y],
        back_same.at[role, y],
        ref["core"].at[2],
        ref["core"].at[3],
        device(1 - role, zh, y, z, x),
    )
    own_back = pltpu.make_async_copy(made_same.at[role, y], back_same.at[role, y], ref["core"].at[4])
    own_back.start()

    gather = PlaneGather(here, got_cross, lane_half, *[ref[f"c{i}"] for i in range(6)])
    sums = PlaneSum(here, made_cross, lane_half, *[ref[f"d{i}"] for i in range(11)], own_first=True)

    def cross_step(i):
        gather.complete(i)
        cross_experts(gather.order[i])
        sums.begin(i)

    for one in swaps:
        one.wait_recv()
    gather.begin()
    gather.pass_on(0)
    gather.start(1)
    gather.pass_on(1)
    column_step(1)
    gather.start(2)
    cross_step(0)
    gather.pass_on(2)
    gather.start(3)
    column_step(3)
    gather.pass_on(3)
    cross_step(1)
    sums.middle(0)
    column_step(2)
    sums.end(0)
    cross_step(2)
    sums.middle(1)
    sums.end(1)
    cross_step(3)
    sums.middle(2)
    sums.end(2)
    sums.middle(3)
    sums.end(3)
    for h in range(2):
        at = pl.ds(h * (half // 2), half // 2)
        ref["done"][:, at] = sums.total(h).astype(BF16)
        swaps.append(
            send(ref["done"].at[:, at], ref["back_cross"].at[:, at], ref["swap"].at[2, h], ref["swap"].at[3, h], source)
        )

    core_back.wait_recv()
    own_back.wait()
    for d in (1, 3, 2):
        for q in range(2):
            arrived(back_same.at[q, (y + d) % 4], ref["back"].at[1, d - 1, q])
    swaps[2].wait_recv()
    swaps[3].wait_recv()
    branches = ref["branches"]
    per_half = half // tile
    for i in range(width // tile):
        at = pl.ds(i * tile, tile)
        table = back_same[:, :, :, at].reshape(8 * UNIT, tile)
        value = dot(ref["shared_act"][...], ref["shared_out"][:, at])
        value = value + dot(ref["gate_high"][...], table) + dot(ref["gate_low"][...], table)
        table = ref["back_cross"][:, pl.ds((i % per_half) * tile, tile)]
        routed = dot(ref["cross_high"][...], table) + dot(ref["cross_low"][...], table)
        value = value + jnp.where(cross_half == i // per_half, routed, 0.0)
        branches[at, :] = value.T.astype(BF16)

    last = PlaneSum(here, branches, flat_half, *[ref[f"e{i}"] for i in range(11)])
    last.whole()
    for h in range(2):
        value = last.total(h) + flat_half(hidden, mine, h)[...].astype(F32)
        out[pl.ds(h * step, step), :] = value.astype(BF16)

    for one in (first, sums, last):
        one.drain()
    gather.finish()
    for one in sent + swaps + [core, core_back]:
        one.wait_send()


def layer_scratch(rows, width, units, tp_count):
    half, part = width // 2, width // tp_count
    small, large = (part // 2, rows), (UNIT, half // 2)
    dma, vmem = pltpu.SemaphoreType.DMA, pltpu.VMEM
    named = {
        "gate": vmem((2 * units, width), BF16),
        "up": vmem((2 * units, width), BF16),
        "down": vmem((2 * units, width), BF16),
        "shared_in": vmem((2, units, width), BF16),
        "shared_out": vmem((units, width), BF16),
        "load": dma((9,)),
        "hidden": vmem((width, rows), BF16),
        "normed": vmem((rows, width), BF16),
        "cross": vmem((UNIT, half), BF16),
        "got_cross": vmem((tp_count, UNIT, half), BF16),
        "made_cross": vmem((tp_count, UNIT, half), BF16),
        "done": vmem((UNIT, half), BF16),
        "back_cross": vmem((UNIT, half), BF16),
        "same": vmem((2, 4, UNIT, width), BF16),
        "got_same": vmem((2, 4, UNIT, width), BF16),
        "made_same": vmem((2, 4, UNIT, width), BF16),
        "back_same": vmem((2, 4, UNIT, width), BF16),
        "weights": vmem((8 * UNIT, rows), F32),
        "gate_high": vmem((rows, 8 * UNIT), BF16),
        "gate_low": vmem((rows, 8 * UNIT), BF16),
        "cross_high": vmem((rows, UNIT), BF16),
        "cross_low": vmem((rows, UNIT), BF16),
        "shared_act": vmem((rows, units), BF16),
        "branches": vmem((width, rows), BF16),
        "swap": dma((4, 2)),
        "near": dma((2, 3, 2)),
        "back": dma((2, 3, 2)),
        "core": dma((5,)),
    }
    for letter, some in (
        ("a", plane_sum_scratch(small)),
        ("b", plane_gather_scratch()),
        ("c", plane_gather_scratch()),
        ("d", plane_sum_scratch(large)),
        ("e", plane_sum_scratch(small)),
    ):
        named.update({f"{letter}{i}": one for i, one in enumerate(some)})
    return list(named), list(named.values())


def body(
    residual,
    queries,
    kv_cache,
    cache_lengths,
    out_proj,
    norm_gain,
    routes,
    gate_weights,
    expert_in,
    expert_out,
    shared_in,
    shared_out,
):
    rows = residual.shape[1]
    part = residual.shape[2]
    tp_count = lax.axis_size("tp")
    width = part * tp_count
    head_count = queries.shape[2] // HD

    query_heads = queries.reshape(rows, head_count, HD)
    cache_rows = kv_cache.reshape(rows, L, 2 * HD)
    cache_keys = cache_rows[:, :, :HD]
    cache_values = cache_rows[:, :, HD:]
    scores = jnp.einsum("rhd,rld->rhl", query_heads, cache_keys, preferred_element_type=F32) * HD ** (-0.5)
    visible = jnp.arange(L, dtype=jnp.int32)[None, None, :] < cache_lengths.reshape(rows)[:, None, None]
    scores = jnp.where(visible, scores, -1e30)
    maximum = jnp.max(scores, axis=-1, keepdims=True)
    exponent = jnp.where(visible, jnp.exp(scores - maximum), 0.0)
    attn_weights = (exponent / jnp.sum(exponent, axis=-1, keepdims=True)).astype(BF16)
    context = jnp.einsum("rhl,rld->rhd", attn_weights, cache_values, preferred_element_type=F32).astype(BF16)
    context = context.reshape(rows, head_count * HD)
    attended = jnp.einsum("kd,rk->dr", out_proj, context, preferred_element_type=F32).astype(BF16)

    names, scratch = layer_scratch(rows, width, expert_out.shape[1], tp_count)
    vmem, hbm = pl.BlockSpec(memory_space=pltpu.VMEM), pl.BlockSpec(memory_space=pl.ANY)
    layer_out = pl.pallas_call(
        functools.partial(layer_kernel, names),
        out_shape=jax.ShapeDtypeStruct((part, rows), BF16),
        in_specs=[vmem] * 5 + [hbm] * 4,
        out_specs=vmem,
        scratch_shapes=scratch,
        compiler_params=pltpu.CompilerParams(collective_id=1, has_side_effects=True, vmem_limit_bytes=VMEM_LIMIT),
    )(
        attended,
        residual.reshape(rows, part).T,
        norm_gain.astype(F32).reshape(1, width),
        routes.reshape(rows, TOPK).T,
        gate_weights.reshape(rows, TOPK).T,
        expert_in,
        expert_out,
        shared_in,
        shared_out,
    )
    return layer_out.T.reshape(1, rows, part)


def solution(mesh):
    in_specs = (
        P("role", "grp", "tp"),
        P("role", "grp", "tp"),
        P("role", "grp", None, None),
        P("role", "grp"),
        P("tp", None),
        P(),
        P("role", "grp", None),
        P("role", "grp", None),
        P(("role", "grp"), None, "tp", None),
        P(("role", "grp"), "tp", None),
        P(None, "tp", None),
        P("tp", None),
    )
    out_specs = P("role", "grp", "tp")
    return jax.shard_map(body, mesh=mesh, in_specs=in_specs, out_specs=out_specs, check_vma=False)
```

```python
import functools

import jax
import jax.numpy as jnp
from jax import lax
from jax.experimental import pallas as pl
from jax.experimental.pallas import tpu as pltpu
from jax.sharding import PartitionSpec as P

HD = 128
EXPERTS = 32
TOPK = 3
L = 16
CAP = 24
UNIT = 2 * CAP
MESH = pl.DeviceIdType.MESH
BF16 = jnp.bfloat16
F32 = jnp.float32
VMEM_LIMIT = 50 * 1024 * 1024


def places():
    role, grp, tp = lax.axis_index("role"), lax.axis_index("grp"), lax.axis_index("tp")
    return role, grp // 4, grp % 4, tp // 4, tp % 4


def flip(a, b):
    return (a + b) % 2


def xor4(a, b):
    return 2 * flip(a // 2, b // 2) + flip(a % 2, b % 2)


def z_mates(z):
    return {1: xor4(z, 1), 2: (z + 2) % 4, 3: 3 - z}


def device(role, zh, y, z, x):
    return {"role": role, "grp": zh * 4 + y, "tp": z * 4 + x}


def partners(role, zh, y, z, x):
    there = (flip(role, x % 2), 1 - zh)
    return device(*there, xor4(y, z), 3 - z, x), device(*there, xor4(y, 3 - z), 3 - z, x)


def plane_mates(role, zh, y, z, x):
    mates = [device(role, zh, y, z, (x + 1) % 4), device(role, zh, y, z, (x + 3) % 4)]
    return mates + [device(role, zh, y, one, x) for one in z_mates(z).values()]


def column_mates(role, zh, y, z, x):
    mates = [device(one, zh, (y + step) % 4, z, x) for step in (1, 2, 3) for one in (0, 1)]
    return mates + [device(1 - role, zh, y, z, x)]


def remote(src, dst, send_sem, recv_sem, to):
    return pltpu.make_async_remote_copy(
        src_ref=src, dst_ref=dst, send_sem=send_sem, recv_sem=recv_sem, device_id=to, device_id_type=MESH
    )


def send(src, dst, send_sem, recv_sem, to):
    copy = remote(src, dst, send_sem, recv_sem, to)
    copy.start()
    return copy


class PlaneSum:
    def __init__(self, here, part, half, rx1, tx, rx2, zt, zrx, s1, r1, s2, r2, zs, zr, own_first=False):
        self.here, self.part, self.half = here, part, half
        self.rx1, self.tx, self.rx2, self.zt, self.zrx = rx1, tx, rx2, zt, zrx
        self.s1, self.r1, self.s2, self.r2, self.zs, self.zr = s1, r1, s2, r2, zs, zr
        role, zh, y, z, x = here
        mates = z_mates(z)
        self.order = [z, mates[2], mates[3], mates[1]] if own_first else [mates[2], mates[3], mates[1], z]
        self.own = 0 if own_first else 3
        self.zslot = {i: n for n, i in enumerate(i for i in range(4) if i != self.own)}
        self.right, self.left = (x + 1) % 4, (x + 3) % 4
        self.to_right = device(role, zh, y, z, self.right)
        self.to_left = device(role, zh, y, z, self.left)
        self.copies = []
        self.first, self.second, self.zcopies = {}, {}, {}

    def begin(self, i):
        x = self.here[4]
        far = (x + 2) % 4
        base = self.order[i] * 4
        for d, (to, near) in enumerate(((self.to_right, self.right), (self.to_left, self.left))):
            self.first[i, d] = send(
                self.half(self.part, base + far, d), self.rx1.at[i, d], self.s1.at[i, d], self.r1.at[i, d], to
            )
            self.second[i, d, 1 - d] = send(
                self.half(self.part, base + near, 1 - d),
                self.rx2.at[i, d, 1 - d],
                self.s2.at[i, d, 1 - d],
                self.r2.at[i, d, 1 - d],
                to,
            )

    def middle(self, i):
        base = self.order[i] * 4
        for d, (to, near) in enumerate(((self.to_right, self.right), (self.to_left, self.left))):
            self.first[i, d].wait_recv()
            own = self.half(self.part, base + near, d)[...]
            self.tx[i, d] = (self.rx1[i, d].astype(F32) + own.astype(F32)).astype(BF16)
            self.second[i, d, d] = send(
                self.tx.at[i, d], self.rx2.at[i, d, d], self.s2.at[i, d, d], self.r2.at[i, d, d], to
            )

    def line(self, i, h):
        x = self.here[4]
        own = self.half(self.part, self.order[i] * 4 + x, h)[...].astype(F32)
        return own + self.rx2[i, 0, h].astype(F32) + self.rx2[i, 1, h].astype(F32)

    def end(self, i):
        role, zh, y, z, x = self.here
        n = self.zslot.get(i)
        for h in range(2):
            for d in range(2):
                self.second[i, d, h].wait_recv()
            if i == self.own:
                continue
            self.zt[n, h] = self.line(i, h).astype(BF16)
            self.zcopies[n, h] = send(
                self.zt.at[n, h],
                self.zrx.at[n, h],
                self.zs.at[n, h],
                self.zr.at[n, h],
                device(role, zh, y, self.order[i], x),
            )

    def total(self, h):
        value = self.line(self.own, h)
        for i in range(3):
            self.zcopies[i, h].wait_recv()
            value = value + self.zrx[i, h].astype(F32)
        return value

    def drain(self):
        for copy in list(self.first.values()) + list(self.second.values()) + list(self.zcopies.values()):
            copy.wait_send()

    def whole(self, between=lambda: None):
        for i in range(4):
            self.begin(i)
        self.middle(0)
        self.middle(1)
        between()
        self.end(0)
        self.middle(2)
        self.end(1)
        self.middle(3)
        self.end(2)
        self.end(3)


def plane_sum_scratch(half):
    dma = pltpu.SemaphoreType.DMA
    return [
        pltpu.VMEM((4, 2) + half, BF16),
        pltpu.VMEM((4, 2) + half, BF16),
        pltpu.VMEM((4, 2, 2) + half, BF16),
        pltpu.VMEM((3, 2) + half, BF16),
        pltpu.VMEM((3, 2) + half, BF16),
        dma((4, 2)),
        dma((4, 2)),
        dma((4, 2, 2)),
        dma((4, 2, 2)),
        dma((3, 2)),
        dma((3, 2)),
    ]


class PlaneGather:
    def __init__(self, here, out, half, zs, zr, xs, xr, fs, fr, ls=None):
        self.here, self.out, self.half, self.ls = here, out, half, ls
        self.zs, self.zr, self.xs, self.xr, self.fs, self.fr = zs, zr, xs, xr, fs, fr
        role, zh, y, z, x = here
        mates = z_mates(z)
        self.order = [z, mates[1], mates[2], mates[3]]
        self.inner = ((z + 1) // 2) % 2 == 1
        self.relays = []
        self.to_right = device(role, zh, y, z, (x + 1) % 4)
        self.to_left = device(role, zh, y, z, (x + 3) % 4)
        self.zcopies, self.near, self.far = {}, {}, {}

    def begin(self, halves=(0, 1)):
        role, zh, y, z, x = self.here
        mine = z * 4 + x
        for h in halves:
            self.spread(0, h)
            block = self.half(self.out, mine, h)
            for m in (1, 2, 3):
                copy = remote(
                    block, block, self.zs.at[m - 1, h], self.zr.at[m - 1, h], device(role, zh, y, self.order[m], x)
                )
                self.zcopies[m, h] = copy
                if m == 3 and self.ls is not None:
                    pl.when(self.inner)(copy.start)
                else:
                    copy.start()

    def spread(self, i, h):
        block = self.half(self.out, self.order[i] * 4 + self.here[4], h)
        for d, to in ((h, (self.to_right, self.to_left)[h]), (1 - h, (self.to_right, self.to_left)[1 - h])):
            self.near[i, d, h] = send(block, block, self.xs.at[i, d, h], self.xr.at[i, d, h], to)

    def start(self, i):
        for h in range(2):
            self.zcopies[i, h].wait_recv()
            self.spread(i, h)

    def relay(self):
        role, zh, y, z, x = self.here
        for h in range(2):
            block = self.half(self.out, self.order[2] * 4 + x, h)
            copy = remote(block, block, self.ls.at[h], self.zr.at[2, h], device(role, zh, y, self.order[1], x))
            pl.when(self.inner)(copy.start)
            self.relays.append(copy)

    def pass_on(self, i):
        x = self.here[4]
        base = self.order[i] * 4
        for d, (to, slot) in enumerate(((self.to_right, (x + 3) % 4), (self.to_left, (x + 1) % 4))):
            self.near[i, d, d].wait_recv()
            block = self.half(self.out, base + slot, d)
            self.far[i, d] = send(block, block, self.fs.at[i, d], self.fr.at[i, d], to)

    def complete(self, i):
        for d in range(2):
            self.near[i, d, 1 - d].wait_recv()
            self.far[i, d].wait_recv()

    def finish(self):
        for copies in (self.near, self.far):
            for copy in copies.values():
                copy.wait_send()
        for (m, h), copy in self.zcopies.items():
            if m == 3 and self.ls is not None:
                pl.when(self.inner)(copy.wait_send)
            else:
                copy.wait_send()
        for copy in self.relays:
            pl.when(self.inner)(copy.wait_send)

    def whole(self, between=lambda: None):
        self.begin()
        self.pass_on(0)
        self.start(1)
        between()
        self.start(2)
        self.pass_on(1)
        self.start(3)
        self.pass_on(2)
        self.pass_on(3)
        for i in range(4):
            self.complete(i)
        self.finish()


def plane_gather_scratch():
    dma = pltpu.SemaphoreType.DMA
    return [dma((3, 2)), dma((3, 2)), dma((4, 2, 2)), dma((4, 2, 2)), dma((4, 2)), dma((4, 2))]


def flat_half(ref, slot, h):
    rows = ref.shape[0] // 32
    return ref.at[pl.ds(pl.multiple_of((2 * slot + h) * rows, 16), rows), :]


def lane_half(ref, slot, h):
    width = ref.shape[2] // 2
    return ref.at[slot, :, pl.ds(h * width, width)]


def dot(a, b):
    return jnp.dot(a, b, preferred_element_type=F32)


def dot_rows(a, b):
    return lax.dot_general(a, b, (((1,), (1,)), ((), ())), preferred_element_type=F32)


def split(value):
    high = value.astype(BF16)
    return high, (value - high.astype(F32)).astype(BF16)


def slot_rows(routes):
    count = routes.shape[1]
    ids = lax.broadcasted_iota(jnp.int32, (EXPERTS, count), 0)
    named = [ids == routes[k : k + 1, :] for k in range(TOPK)]
    chosen = jnp.where(named[0] | named[1] | named[2], 1.0, 0.0).astype(BF16)
    earlier = lax.broadcasted_iota(jnp.int32, (count, count), 0) < lax.broadcasted_iota(jnp.int32, (count, count), 1)
    before = dot(chosen, jnp.where(earlier, 1.0, 0.0).astype(BF16))
    place = [jnp.sum(jnp.where(one, before, 0.0), axis=0, keepdims=True).astype(jnp.int32) for one in named]
    return [routes[k : k + 1, :] * CAP + place[k] for k in range(TOPK)]


def unit_hits(slots, owner):
    ids = lax.broadcasted_iota(jnp.int32, (UNIT, slots[0].shape[1]), 0) + owner * UNIT
    return [ids == one for one in slots]


def layer_kernel(names, part, resid, gain, routes, gates, w_in, w_out, s_in, s_out, out, *scratch):
    ref = dict(zip(names, scratch))
    here = places()
    role, zh, y, z, x = here
    mine = z * 4 + x
    rows = routes.shape[1]
    width = gain.shape[1]
    half = width // 2
    units = w_in.shape[2]
    to, source = partners(*here)

    barrier = pltpu.get_barrier_semaphore()
    mates = plane_mates(*here) + column_mates(*here) + [to, source]
    for one in mates:
        pl.semaphore_signal(barrier, inc=1, device_id=one, device_id_type=MESH)

    loads = []
    for j in range(2):
        loads.append((w_in.at[j, 0], ref["gate"].at[pl.ds(j * units, units), :]))
        loads.append((w_in.at[j, 1], ref["up"].at[pl.ds(j * units, units), :]))
        loads.append((w_out.at[j], ref["down"].at[pl.ds(j * units, units), :]))
        loads.append((s_in.at[j], ref["shared_in"].at[j]))
    loads.append((s_out, ref["shared_out"]))
    loads = [pltpu.make_async_copy(a, b, ref["load"].at[i]) for i, (a, b) in enumerate(loads)]
    for one in loads:
        one.start()

    slots = slot_rows(routes[...])
    gate_rows = gates[...]

    def pick(owner):
        hits = unit_hits(slots, owner)
        return jnp.where(hits[0] | hits[1] | hits[2], 1.0, 0.0).astype(BF16)

    def weigh(owner):
        hits = unit_hits(slots, owner)
        return sum(jnp.where(hits[k], gate_rows[k : k + 1, :], 0.0) for k in range(TOPK))

    def owner_of(q, yo):
        return q * 8 + zh * 4 + yo

    cross_owner = flip(role, x % 2) * 8 + (1 - zh) * 4 + xor4(y, z)
    cross_half = x // 2

    pl.semaphore_wait(barrier, len(mates))
    first = PlaneSum(here, part, flat_half, *[ref[f"a{i}"] for i in range(11)])
    first.whole()
    hidden = ref["hidden"]
    step = resid.shape[0] // 2
    for h in range(2):
        value = first.total(h) + resid[pl.ds(h * step, step), :].astype(F32)
        flat_half(hidden, mine, h)[...] = value.astype(BF16)
    PlaneGather(here, hidden, flat_half, *[ref[f"b{i}"] for i in range(6)]).whole()

    normed = ref["normed"]
    tile = 256
    square = jnp.zeros((rows, 1), F32)
    for i in range(width // tile):
        wide = hidden[pl.ds(i * tile, tile), :].astype(F32).T
        square = square + jnp.sum(wide * wide, axis=1, keepdims=True)
        normed[:, pl.ds(i * tile, tile)] = wide.astype(BF16)
    scale = lax.rsqrt(square / width + 1e-06)
    for i in range(width // tile):
        at = pl.ds(i * tile, tile)
        normed[:, at] = (normed[:, at].astype(F32) * scale * gain[:, at]).astype(BF16)

    chosen = pick(cross_owner)
    got_cross = ref["got_cross"]
    swaps = []
    for h in range(2):
        at = pl.ds(h * (half // 2), half // 2)
        from_at = pl.ds(pl.multiple_of(cross_half * half + h * (half // 2), 128), half // 2)
        ref["cross"][:, at] = dot(chosen, normed[:, from_at]).astype(BF16)
        swaps.append(
            send(
                ref["cross"].at[:, at],
                got_cross.at[(3 - z) * 4 + x, :, at],
                ref["swap"].at[0, h],
                ref["swap"].at[1, h],
                to,
            )
        )
    same, got_same, back_same = ref["same"], ref["got_same"], ref["back_same"]
    sent = []

    def pick_into(target, owner):
        chosen = pick(owner)
        for h in range(4):
            at = pl.ds(h * (width // 4), width // 4)
            target[:, at] = dot(chosen, normed[:, at]).astype(BF16)

    pick_into(same.at[1 - role, y], owner_of(1 - role, y))
    core = send(
        same.at[1 - role, y], got_same.at[role, y], ref["core"].at[0], ref["core"].at[1], device(1 - role, zh, y, z, x)
    )
    pick_into(got_same.at[role, y], owner_of(role, y))

    for one in loads:
        one.wait()

    for q in range(2):
        for yo in range(4):
            at = pl.ds((q * 4 + yo) * UNIT, UNIT)
            ref["weights"][at, :] = weigh(owner_of(q, yo))
    ref["gate_high"][...], ref["gate_low"][...] = split(ref["weights"][...].T)
    ref["cross_high"][...], ref["cross_low"][...] = split(weigh(cross_owner).T)
    pre = [dot_rows(normed[...], ref["shared_in"][g]) for g in range(2)]
    ref["shared_act"][...] = (jax.nn.silu(pre[0]) * pre[1]).astype(BF16)

    both = 2 * UNIT
    inner = (lax.broadcasted_iota(jnp.int32, (both, 2 * units), 0) % UNIT) >= CAP
    second = lax.broadcasted_iota(jnp.int32, (both, 2 * units), 1) >= units
    own_expert = jnp.logical_not(jnp.logical_xor(inner, second))

    def experts(load, store):
        at = [pl.ds(h * half, half) for h in range(2)]
        found = [load(h) for h in range(2)]
        gate_pre = sum(dot_rows(found[h], ref["gate"][:, at[h]]) for h in range(2))
        up_pre = sum(dot_rows(found[h], ref["up"][:, at[h]]) for h in range(2))
        act = jnp.where(own_expert, jax.nn.silu(gate_pre) * up_pre, 0.0).astype(BF16)
        for h in range(2):
            for c in range(2):
                columns = pl.ds(h * half + c * (half // 2), half // 2)
                result = dot(act, ref["down"][:, columns]).astype(BF16)
                store(h, c, result.reshape(2, UNIT, half // 2))

    made_same, made_cross = ref["made_same"], ref["made_cross"]

    def same_experts(yo):
        def load(h):
            return got_same[:, yo, :, pl.ds(h * half, half)].reshape(both, half)

        def store(h, c, value):
            made_same[:, yo, :, pl.ds(h * half + c * (half // 2), half // 2)] = value

        experts(load, store)

    def cross_experts(zz):
        def load(h):
            return got_cross[pl.ds(zz * 4 + 2 * h, 2)].reshape(both, half)

        def store(h, c, value):
            made_cross[pl.ds(zz * 4 + 2 * h, 2), :, pl.ds(c * (half // 2), half // 2)] = value

        experts(load, store)

    def arrived(block, sem):
        pltpu.make_async_copy(block, block, sem).wait()

    def column_step(d):
        yo = (y + 4 - d) % 4
        for q in range(2):
            arrived(got_same.at[q, yo], ref["near"].at[1, d - 1, q])
        same_experts(yo)
        for q in range(2):
            sent.append(
                send(
                    made_same.at[q, yo],
                    back_same.at[role, y],
                    ref["back"].at[0, d - 1, q],
                    ref["back"].at[1, d - 1, role],
                    device(q, zh, yo, z, x),
                )
            )

    core.wait_recv()
    same_experts(y)
    core_back = send(
        made_same.at[1 - role, y],
        back_same.at[role, y],
        ref["core"].at[2],
        ref["core"].at[3],
        device(1 - role, zh, y, z, x),
    )
    own_back = pltpu.make_async_copy(made_same.at[role, y], back_same.at[role, y], ref["core"].at[4])
    own_back.start()

    for d in (1, 3, 2):
        yo = (y + d) % 4
        for q in range(2):
            pick_into(same.at[q, yo], owner_of(q, yo))
            sent.append(
                send(
                    same.at[q, yo],
                    got_same.at[role, y],
                    ref["near"].at[0, d - 1, q],
                    ref["near"].at[1, d - 1, role],
                    device(q, zh, yo, z, x),
                )
            )

    gather = PlaneGather(here, got_cross, lane_half, *[ref[f"c{i}"] for i in range(6)], ls=ref["relay"])
    sums = PlaneSum(here, made_cross, lane_half, *[ref[f"d{i}"] for i in range(11)], own_first=True)

    def cross_step(i):
        gather.complete(i)
        cross_experts(gather.order[i])

    for h in range(2):
        swaps[h].wait_recv()
        gather.begin((h,))
    gather.pass_on(0)
    gather.start(1)
    gather.pass_on(1)
    gather.start(2)
    gather.relay()
    cross_step(0)
    sums.begin(0)
    gather.pass_on(2)
    gather.start(3)
    cross_step(1)
    sums.middle(0)
    gather.pass_on(3)
    column_step(1)
    cross_step(2)
    sums.begin(1)
    column_step(3)
    cross_step(3)
    sums.begin(2)
    sums.middle(1)
    sums.begin(3)
    sums.end(1)
    sums.middle(2)
    sums.end(2)
    sums.middle(3)
    column_step(2)
    sums.end(0)
    sums.end(3)
    for h in range(2):
        at = pl.ds(h * (half // 2), half // 2)
        ref["done"][:, at] = sums.total(h).astype(BF16)
        swaps.append(
            send(ref["done"].at[:, at], ref["back_cross"].at[:, at], ref["swap"].at[2, h], ref["swap"].at[3, h], source)
        )

    core_back.wait_recv()
    own_back.wait()
    for d in (1, 3, 2):
        for q in range(2):
            arrived(back_same.at[q, (y + d) % 4], ref["back"].at[1, d - 1, q])
    swaps[2].wait_recv()
    swaps[3].wait_recv()
    branches = ref["branches"]
    last = PlaneSum(here, branches, flat_half, *[ref[f"e{i}"] for i in range(11)])
    quarter = width // 4

    def combine(i):
        zz = last.order[i]
        start = 0
        for size in (256, 256, 384):
            at = pl.ds(pl.multiple_of(zz * quarter + start, 128), size)
            table = back_same[:, :, :, at].reshape(8 * UNIT, size)
            value = dot(ref["shared_act"][...], ref["shared_out"][:, at])
            value = value + dot(ref["gate_high"][...], table) + dot(ref["gate_low"][...], table)
            table = ref["back_cross"][:, pl.ds(pl.multiple_of((zz % 2) * quarter + start, 128), size)]
            routed = dot(ref["cross_high"][...], table) + dot(ref["cross_low"][...], table)
            value = value + jnp.where(cross_half == zz // 2, routed, 0.0)
            branches[at, :] = value.T.astype(BF16)
            start += size
        last.begin(i)

    combine(0)
    combine(1)
    last.middle(0)
    combine(2)
    last.middle(1)
    combine(3)
    last.end(0)
    last.middle(2)
    last.end(1)
    last.middle(3)
    last.end(2)
    last.end(3)
    for h in range(2):
        value = last.total(h) + flat_half(hidden, mine, h)[...].astype(F32)
        out[pl.ds(h * step, step), :] = value.astype(BF16)

    for one in (first, sums, last):
        one.drain()
    gather.finish()
    for one in sent + swaps + [core, core_back]:
        one.wait_send()


def layer_scratch(rows, width, units, tp_count):
    half, part = width // 2, width // tp_count
    small, large = (part // 2, rows), (UNIT, half // 2)
    dma, vmem = pltpu.SemaphoreType.DMA, pltpu.VMEM
    named = {
        "gate": vmem((2 * units, width), BF16),
        "up": vmem((2 * units, width), BF16),
        "down": vmem((2 * units, width), BF16),
        "shared_in": vmem((2, units, width), BF16),
        "shared_out": vmem((units, width), BF16),
        "load": dma((9,)),
        "hidden": vmem((width, rows), BF16),
        "normed": vmem((rows, width), BF16),
        "cross": vmem((UNIT, half), BF16),
        "got_cross": vmem((tp_count, UNIT, half), BF16),
        "made_cross": vmem((tp_count, UNIT, half), BF16),
        "done": vmem((UNIT, half), BF16),
        "back_cross": vmem((UNIT, half), BF16),
        "same": vmem((2, 4, UNIT, width), BF16),
        "got_same": vmem((2, 4, UNIT, width), BF16),
        "made_same": vmem((2, 4, UNIT, width), BF16),
        "back_same": vmem((2, 4, UNIT, width), BF16),
        "weights": vmem((8 * UNIT, rows), F32),
        "gate_high": vmem((rows, 8 * UNIT), BF16),
        "gate_low": vmem((rows, 8 * UNIT), BF16),
        "cross_high": vmem((rows, UNIT), BF16),
        "cross_low": vmem((rows, UNIT), BF16),
        "shared_act": vmem((rows, units), BF16),
        "branches": vmem((width, rows), BF16),
        "swap": dma((4, 2)),
        "relay": dma((2,)),
        "near": dma((2, 3, 2)),
        "back": dma((2, 3, 2)),
        "core": dma((5,)),
    }
    for letter, some in (
        ("a", plane_sum_scratch(small)),
        ("b", plane_gather_scratch()),
        ("c", plane_gather_scratch()),
        ("d", plane_sum_scratch(large)),
        ("e", plane_sum_scratch(small)),
    ):
        named.update({f"{letter}{i}": one for i, one in enumerate(some)})
    return list(named), list(named.values())


def body(
    residual,
    queries,
    kv_cache,
    cache_lengths,
    out_proj,
    norm_gain,
    routes,
    gate_weights,
    expert_in,
    expert_out,
    shared_in,
    shared_out,
):
    rows = residual.shape[1]
    part = residual.shape[2]
    tp_count = lax.axis_size("tp")
    width = part * tp_count
    head_count = queries.shape[2] // HD

    query_heads = queries.reshape(rows, head_count, HD)
    cache_rows = kv_cache.reshape(rows, L, 2 * HD)
    cache_keys = cache_rows[:, :, :HD]
    cache_values = cache_rows[:, :, HD:]
    scores = jnp.einsum("rhd,rld->rhl", query_heads, cache_keys, preferred_element_type=F32) * HD ** (-0.5)
    visible = jnp.arange(L, dtype=jnp.int32)[None, None, :] < cache_lengths.reshape(rows)[:, None, None]
    scores = jnp.where(visible, scores, -1e30)
    maximum = jnp.max(scores, axis=-1, keepdims=True)
    exponent = jnp.where(visible, jnp.exp(scores - maximum), 0.0)
    attn_weights = (exponent / jnp.sum(exponent, axis=-1, keepdims=True)).astype(BF16)
    context = jnp.einsum("rhl,rld->rhd", attn_weights, cache_values, preferred_element_type=F32).astype(BF16)
    context = context.reshape(rows, head_count * HD)
    attended = jnp.einsum("kd,rk->dr", out_proj, context, preferred_element_type=F32).astype(BF16)

    names, scratch = layer_scratch(rows, width, expert_out.shape[1], tp_count)
    vmem, hbm = pl.BlockSpec(memory_space=pltpu.VMEM), pl.BlockSpec(memory_space=pl.ANY)
    layer_out = pl.pallas_call(
        functools.partial(layer_kernel, names),
        out_shape=jax.ShapeDtypeStruct((part, rows), BF16),
        in_specs=[vmem] * 5 + [hbm] * 4,
        out_specs=vmem,
        scratch_shapes=scratch,
        compiler_params=pltpu.CompilerParams(collective_id=1, has_side_effects=True, vmem_limit_bytes=VMEM_LIMIT),
    )(
        attended,
        residual.reshape(rows, part).T,
        norm_gain.astype(F32).reshape(1, width),
        routes.reshape(rows, TOPK).T,
        gate_weights.reshape(rows, TOPK).T,
        expert_in,
        expert_out,
        shared_in,
        shared_out,
    )
    return layer_out.T.reshape(1, rows, part)


def solution(mesh):
    in_specs = (
        P("role", "grp", "tp"),
        P("role", "grp", "tp"),
        P("role", "grp", None, None),
        P("role", "grp"),
        P("tp", None),
        P(),
        P("role", "grp", None),
        P("role", "grp", None),
        P(("role", "grp"), None, "tp", None),
        P(("role", "grp"), "tp", None),
        P(None, "tp", None),
        P("tp", None),
    )
    out_specs = P("role", "grp", "tp")
    return jax.shard_map(body, mesh=mesh, in_specs=in_specs, out_specs=out_specs, check_vma=False)
```

```python
import functools

import jax
import jax.numpy as jnp
from jax import lax
from jax.experimental import pallas as pl
from jax.experimental.pallas import tpu as pltpu
from jax.sharding import PartitionSpec as P

HD = 128
EXPERTS = 32
TOPK = 3
L = 16
CAP = 24
UNIT = 2 * CAP
MESH = pl.DeviceIdType.MESH
BF16 = jnp.bfloat16
F32 = jnp.float32
VMEM_LIMIT = 63 * 1024 * 1024


def places():
    role, grp, tp = lax.axis_index("role"), lax.axis_index("grp"), lax.axis_index("tp")
    return role, grp // 4, grp % 4, tp // 4, tp % 4


def flip(a, b):
    return (a + b) % 2


def xor4(a, b):
    return 2 * flip(a // 2, b // 2) + flip(a % 2, b % 2)


def z_mates(z):
    return {1: xor4(z, 1), 2: (z + 2) % 4, 3: 3 - z}


def device(role, zh, y, z, x):
    return {"role": role, "grp": zh * 4 + y, "tp": z * 4 + x}


def partners(role, zh, y, z, x):
    there = (flip(role, x % 2), 1 - zh)
    return device(*there, xor4(y, z), 3 - z, x), device(*there, xor4(y, 3 - z), 3 - z, x)


def plane_mates(role, zh, y, z, x):
    mates = [device(role, zh, y, z, (x + 1) % 4), device(role, zh, y, z, (x + 3) % 4)]
    return mates + [device(role, zh, y, one, x) for one in z_mates(z).values()]


def column_mates(role, zh, y, z, x):
    mates = [device(one, zh, (y + step) % 4, z, x) for step in (1, 2, 3) for one in (0, 1)]
    return mates + [device(1 - role, zh, y, z, x)]


def remote(src, dst, send_sem, recv_sem, to):
    return pltpu.make_async_remote_copy(
        src_ref=src, dst_ref=dst, send_sem=send_sem, recv_sem=recv_sem, device_id=to, device_id_type=MESH
    )


def send(src, dst, send_sem, recv_sem, to):
    copy = remote(src, dst, send_sem, recv_sem, to)
    copy.start()
    return copy


class PlaneSum:
    def __init__(self, here, part, half, rx1, tx, rx2, zt, zrx, s1, r1, s2, r2, zs, zr, own_first=False):
        self.here, self.part, self.half = here, part, half
        self.rx1, self.tx, self.rx2, self.zt, self.zrx = rx1, tx, rx2, zt, zrx
        self.s1, self.r1, self.s2, self.r2, self.zs, self.zr = s1, r1, s2, r2, zs, zr
        role, zh, y, z, x = here
        mates = z_mates(z)
        self.order = [z, mates[2], mates[3], mates[1]] if own_first else [mates[2], mates[3], mates[1], z]
        self.own = 0 if own_first else 3
        self.zslot = {i: n for n, i in enumerate(i for i in range(4) if i != self.own)}
        self.right, self.left = (x + 1) % 4, (x + 3) % 4
        self.to_right = device(role, zh, y, z, self.right)
        self.to_left = device(role, zh, y, z, self.left)
        self.copies = []
        self.first, self.second, self.zcopies = {}, {}, {}

    def begin(self, i):
        x = self.here[4]
        far = (x + 2) % 4
        base = self.order[i] * 4
        for d, (to, near) in enumerate(((self.to_right, self.right), (self.to_left, self.left))):
            self.first[i, d] = send(
                self.half(self.part, base + far, d), self.rx1.at[i, d], self.s1.at[i, d], self.r1.at[i, d], to
            )
            self.second[i, d, 1 - d] = send(
                self.half(self.part, base + near, 1 - d),
                self.rx2.at[i, d, 1 - d],
                self.s2.at[i, d, 1 - d],
                self.r2.at[i, d, 1 - d],
                to,
            )

    def middle(self, i):
        base = self.order[i] * 4
        for d, (to, near) in enumerate(((self.to_right, self.right), (self.to_left, self.left))):
            self.first[i, d].wait_recv()
            own = self.half(self.part, base + near, d)[...]
            self.tx[i, d] = (self.rx1[i, d].astype(F32) + own.astype(F32)).astype(BF16)
            self.second[i, d, d] = send(
                self.tx.at[i, d], self.rx2.at[i, d, d], self.s2.at[i, d, d], self.r2.at[i, d, d], to
            )

    def line(self, i, h):
        x = self.here[4]
        own = self.half(self.part, self.order[i] * 4 + x, h)[...].astype(F32)
        return own + self.rx2[i, 0, h].astype(F32) + self.rx2[i, 1, h].astype(F32)

    def end(self, i):
        role, zh, y, z, x = self.here
        n = self.zslot.get(i)
        for h in range(2):
            for d in range(2):
                self.second[i, d, h].wait_recv()
            if i == self.own:
                continue
            self.zt[n, h] = self.line(i, h).astype(BF16)
            self.zcopies[n, h] = send(
                self.zt.at[n, h],
                self.zrx.at[n, h],
                self.zs.at[n, h],
                self.zr.at[n, h],
                device(role, zh, y, self.order[i], x),
            )

    def total(self, h):
        value = self.line(self.own, h)
        for i in range(3):
            self.zcopies[i, h].wait_recv()
            value = value + self.zrx[i, h].astype(F32)
        return value

    def drain(self):
        for copy in list(self.first.values()) + list(self.second.values()) + list(self.zcopies.values()):
            copy.wait_send()

    def whole(self, between=lambda: None):
        for i in range(4):
            self.begin(i)
        self.middle(0)
        self.middle(1)
        between()
        self.end(0)
        self.middle(2)
        self.end(1)
        self.middle(3)
        self.end(2)
        self.end(3)


def plane_sum_scratch(half):
    dma = pltpu.SemaphoreType.DMA
    return [
        pltpu.VMEM((4, 2) + half, BF16),
        pltpu.VMEM((4, 2) + half, BF16),
        pltpu.VMEM((4, 2, 2) + half, BF16),
        pltpu.VMEM((3, 2) + half, BF16),
        pltpu.VMEM((3, 2) + half, BF16),
        dma((4, 2)),
        dma((4, 2)),
        dma((4, 2, 2)),
        dma((4, 2, 2)),
        dma((3, 2)),
        dma((3, 2)),
    ]


class PlaneGather:
    def __init__(self, here, out, half, zs, zr, xs, xr, fs, fr, ls=None):
        self.here, self.out, self.half, self.ls = here, out, half, ls
        self.zs, self.zr, self.xs, self.xr, self.fs, self.fr = zs, zr, xs, xr, fs, fr
        role, zh, y, z, x = here
        mates = z_mates(z)
        self.order = [z, mates[1], mates[2], mates[3]]
        self.inner = ((z + 1) // 2) % 2 == 1
        self.relays = []
        self.to_right = device(role, zh, y, z, (x + 1) % 4)
        self.to_left = device(role, zh, y, z, (x + 3) % 4)
        self.zcopies, self.near, self.far = {}, {}, {}

    def begin(self, halves=(0, 1)):
        role, zh, y, z, x = self.here
        mine = z * 4 + x
        for h in halves:
            self.spread(0, h)
            block = self.half(self.out, mine, h)
            for m in (1, 2, 3):
                copy = remote(
                    block, block, self.zs.at[m - 1, h], self.zr.at[m - 1, h], device(role, zh, y, self.order[m], x)
                )
                self.zcopies[m, h] = copy
                if m == 3 and self.ls is not None:
                    pl.when(self.inner)(copy.start)
                else:
                    copy.start()

    def spread(self, i, h):
        block = self.half(self.out, self.order[i] * 4 + self.here[4], h)
        for d, to in ((h, (self.to_right, self.to_left)[h]), (1 - h, (self.to_right, self.to_left)[1 - h])):
            self.near[i, d, h] = send(block, block, self.xs.at[i, d, h], self.xr.at[i, d, h], to)

    def start(self, i):
        for h in range(2):
            self.zcopies[i, h].wait_recv()
            self.spread(i, h)

    def relay(self):
        role, zh, y, z, x = self.here
        for h in range(2):
            block = self.half(self.out, self.order[2] * 4 + x, h)
            copy = remote(block, block, self.ls.at[h], self.zr.at[2, h], device(role, zh, y, self.order[1], x))
            pl.when(self.inner)(copy.start)
            self.relays.append(copy)

    def pass_on(self, i):
        x = self.here[4]
        base = self.order[i] * 4
        for d, (to, slot) in enumerate(((self.to_right, (x + 3) % 4), (self.to_left, (x + 1) % 4))):
            self.near[i, d, d].wait_recv()
            block = self.half(self.out, base + slot, d)
            self.far[i, d] = send(block, block, self.fs.at[i, d], self.fr.at[i, d], to)

    def complete(self, i):
        for d in range(2):
            self.near[i, d, 1 - d].wait_recv()
            self.far[i, d].wait_recv()

    def finish(self):
        for copies in (self.near, self.far):
            for copy in copies.values():
                copy.wait_send()
        for (m, h), copy in self.zcopies.items():
            if m == 3 and self.ls is not None:
                pl.when(self.inner)(copy.wait_send)
            else:
                copy.wait_send()
        for copy in self.relays:
            pl.when(self.inner)(copy.wait_send)

    def whole(self, between=lambda: None):
        self.begin()
        self.pass_on(0)
        self.start(1)
        between()
        self.start(2)
        self.pass_on(1)
        self.start(3)
        self.pass_on(2)
        self.pass_on(3)
        for i in range(4):
            self.complete(i)
        self.finish()


def plane_gather_scratch():
    dma = pltpu.SemaphoreType.DMA
    return [dma((3, 2)), dma((3, 2)), dma((4, 2, 2)), dma((4, 2, 2)), dma((4, 2)), dma((4, 2))]


def flat_half(ref, slot, h):
    rows = ref.shape[0] // 32
    return ref.at[pl.ds(pl.multiple_of((2 * slot + h) * rows, 16), rows), :]


def lane_half(ref, slot, h):
    width = ref.shape[2] // 2
    return ref.at[slot, :, pl.ds(h * width, width)]


def dot(a, b):
    return jnp.dot(a, b, preferred_element_type=F32)


def dot_rows(a, b):
    return lax.dot_general(a, b, (((1,), (1,)), ((), ())), preferred_element_type=F32)


def split(value):
    high = value.astype(BF16)
    return high, (value - high.astype(F32)).astype(BF16)


def slot_rows(routes):
    count = routes[0].shape[1]
    ids = lax.broadcasted_iota(jnp.int32, (EXPERTS, count), 0)
    named = [ids == one for one in routes]
    chosen = jnp.where(named[0] | named[1] | named[2], 1.0, 0.0).astype(BF16)
    earlier = lax.broadcasted_iota(jnp.int32, (count, count), 0) < lax.broadcasted_iota(jnp.int32, (count, count), 1)
    before = dot(chosen, jnp.where(earlier, 1.0, 0.0).astype(BF16))
    place = [jnp.sum(jnp.where(one, before, 0.0), axis=0, keepdims=True).astype(jnp.int32) for one in named]
    return [routes[k] * CAP + place[k] for k in range(TOPK)]


def unit_hits(slots, owner):
    ids = lax.broadcasted_iota(jnp.int32, (UNIT, slots[0].shape[1]), 0) + owner * UNIT
    return [ids == one for one in slots]


def same_place(count):
    place = [lax.broadcasted_iota(jnp.int32, (count, count), d) for d in range(2)]
    return jnp.where(place[0] == place[1], 1.0, 0.0).astype(BF16)


def attend(queries, kv, lengths, context):
    rows = queries.shape[0]
    block = 32
    place = [lax.broadcasted_iota(jnp.int32, (rows, rows), d) for d in range(2)]
    live = jnp.where(place[0] == place[1], lengths[...].astype(F32), 0.0)
    live = jnp.sum(live, axis=1, keepdims=True).astype(jnp.int32)
    ahead = lax.broadcasted_iota(jnp.int32, (block, block * L), 1) - L * lax.broadcasted_iota(
        jnp.int32, (block, block * L), 0
    )
    parts = [(start, head) for start in range(0, rows, block) for head in range(queries.shape[1] // HD)]
    scores = [
        dot_rows(queries[start : start + block, head * HD : (head + 1) * HD], kv[start * L : (start + block) * L, :HD])
        * HD ** (-0.5)
        for start, head in parts
    ]
    weights = []
    for (start, _), score in zip(parts, scores):
        visible = (ahead >= 0) & (ahead < live[start : start + block])
        score = jnp.where(visible, score, -1e30)
        maximum = jnp.max(score, axis=1, keepdims=True)
        exponent = jnp.where(visible, jnp.exp(score - maximum), 0.0)
        weights.append((exponent / jnp.sum(exponent, axis=1, keepdims=True)).astype(BF16))
    for (start, head), weight in zip(parts, weights):
        values = kv[start * L : (start + block) * L, HD:]
        context[start : start + block, head * HD : (head + 1) * HD] = dot(weight, values).astype(BF16)


def layer_kernel(
    names, gain, len_in, routes_in, gates_in, q_in, kv_in, resid_in, o_proj, w_in, w_out, s_in, s_out, out, *scratch
):
    ref = dict(zip(names, scratch))
    here = places()
    role, zh, y, z, x = here
    mine = z * 4 + x
    rows = routes_in.shape[2]
    width = gain.shape[0]
    half = width // 2
    units = w_in.shape[2]
    to, source = partners(*here)

    queries, kv, resid = ref["queries"], ref["kv"], ref["resid"]
    loads = [
        (len_in, ref["lengths"]),
        (q_in, queries),
        (kv_in, kv),
        (o_proj, ref["out_proj"]),
        (routes_in, ref["routes"]),
        (gates_in, ref["gates"]),
        (resid_in, resid),
    ]
    for j in range(2):
        loads.append((w_in.at[j, 0], ref["gate"].at[pl.ds(j * units, units), :]))
        loads.append((w_in.at[j, 1], ref["up"].at[pl.ds(j * units, units), :]))
        loads.append((w_out.at[j], ref["down"].at[pl.ds(j * units, units), :]))
        loads.append((s_in.at[j], ref["shared_in"].at[j]))
    loads.append((s_out, ref["shared_out"]))
    loads = [pltpu.make_async_copy(a, b, ref["load"].at[i]) for i, (a, b) in enumerate(loads)]
    for one in loads[:4]:
        one.start()
    barrier = pltpu.get_barrier_semaphore()
    mates = plane_mates(*here) + column_mates(*here) + [to, source]
    for one in mates:
        pl.semaphore_signal(barrier, inc=1, device_id=one, device_id_type=MESH)

    for one in loads[4:]:
        one.start()


    cross_owner = flip(role, x % 2) * 8 + (1 - zh) * 4 + xor4(y, z)
    cross_half = x // 2

    for one in loads[:3]:
        one.wait()
    attend(queries, kv, ref["lengths"], ref["context"])

    eye = same_place(rows)
    quarter = width // 4
    first = PlaneSum(here, ref["attended"], flat_half, *[ref[f"a{i}"] for i in range(11)])
    loads[3].wait()

    def project(i):
        start = 0
        for size in (256, 256, 384):
            at = pl.ds(pl.multiple_of(first.order[i] * quarter + start, 128), size)
            ref["attended"][at, :] = dot(ref["context"][...], ref["out_proj"][:, at]).T.astype(BF16)
            start += size

    project(0)
    pl.semaphore_wait(barrier, len(mates))
    first.begin(0)
    project(1)
    first.begin(1)
    project(2)
    first.begin(2)
    first.middle(0)
    project(3)
    first.begin(3)

    for one in loads[4:7]:
        one.wait()
    slots = slot_rows([ref["routes"][k] for k in range(TOPK)])
    gate_rows = [ref["gates"][k] for k in range(TOPK)]

    def pick(owner):
        hits = unit_hits(slots, owner)
        return jnp.where(hits[0] | hits[1] | hits[2], 1.0, 0.0).astype(BF16)

    def weigh(owner):
        hits = unit_hits(slots, owner)
        return sum(jnp.where(hits[k], gate_rows[k], 0.0) for k in range(TOPK))

    def owner_of(q, yo):
        return q * 8 + zh * 4 + yo

    for q in range(2):
        for yo in range(4):
            at = pl.ds((q * 4 + yo) * UNIT, UNIT)
            ref["weights"][at, :] = weigh(owner_of(q, yo))
    ref["gate_high"][...], ref["gate_low"][...] = split(ref["weights"][...].T)
    ref["cross_high"][...], ref["cross_low"][...] = split(weigh(cross_owner).T)

    first.middle(1)
    first.end(0)
    first.middle(2)
    first.end(1)
    first.middle(3)
    first.end(2)
    first.end(3)
    hidden = ref["hidden"]
    step = resid.shape[0] // 2
    for h in range(2):
        value = first.total(h) + resid[pl.ds(h * step, step), :].astype(F32)
        flat_half(hidden, mine, h)[...] = value.astype(BF16)
    PlaneGather(here, hidden, flat_half, *[ref[f"b{i}"] for i in range(6)]).whole()

    normed = ref["normed"]
    tile = 256
    square = jnp.zeros((rows, 1), F32)
    for i in range(width // tile):
        wide = dot_rows(eye, hidden[pl.ds(i * tile, tile), :])
        square = square + jnp.sum(wide * wide, axis=1, keepdims=True)
        normed[:, pl.ds(i * tile, tile)] = wide.astype(BF16)
    scale = lax.rsqrt(square / width + 1e-06)
    for i in range(width // tile):
        at = pl.ds(i * tile, tile)
        normed[:, at] = (normed[:, at].astype(F32) * scale * gain[at].astype(F32).reshape(1, tile)).astype(BF16)

    chosen = pick(cross_owner)
    got_cross = ref["got_cross"]
    swaps = []
    for h in range(2):
        at = pl.ds(h * (half // 2), half // 2)
        from_at = pl.ds(pl.multiple_of(cross_half * half + h * (half // 2), 128), half // 2)
        ref["cross"][:, at] = dot(chosen, normed[:, from_at]).astype(BF16)
        swaps.append(
            send(
                ref["cross"].at[:, at],
                got_cross.at[(3 - z) * 4 + x, :, at],
                ref["swap"].at[0, h],
                ref["swap"].at[1, h],
                to,
            )
        )
    same, got_same, back_same = ref["same"], ref["got_same"], ref["back_same"]
    sent = []

    def pick_into(target, owner):
        chosen = pick(owner)
        for h in range(4):
            at = pl.ds(h * (width // 4), width // 4)
            target[:, at] = dot(chosen, normed[:, at]).astype(BF16)

    pick_into(same.at[1 - role, y], owner_of(1 - role, y))
    core = send(
        same.at[1 - role, y], got_same.at[role, y], ref["core"].at[0], ref["core"].at[1], device(1 - role, zh, y, z, x)
    )
    pick_into(got_same.at[role, y], owner_of(role, y))

    for one in loads[7:]:
        one.wait()

    pre = [dot_rows(normed[...], ref["shared_in"][g]) for g in range(2)]
    ref["shared_act"][...] = (jax.nn.silu(pre[0]) * pre[1]).astype(BF16)

    both = 2 * UNIT
    inner = (lax.broadcasted_iota(jnp.int32, (both, 2 * units), 0) % UNIT) >= CAP
    second = lax.broadcasted_iota(jnp.int32, (both, 2 * units), 1) >= units
    own_expert = jnp.logical_not(jnp.logical_xor(inner, second))

    def experts(load, store):
        at = [pl.ds(h * half, half) for h in range(2)]
        found = [load(h) for h in range(2)]
        gate_pre = sum(dot_rows(found[h], ref["gate"][:, at[h]]) for h in range(2))
        up_pre = sum(dot_rows(found[h], ref["up"][:, at[h]]) for h in range(2))
        act = jnp.where(own_expert, jax.nn.silu(gate_pre) * up_pre, 0.0).astype(BF16)
        for h in range(2):
            for c in range(2):
                columns = pl.ds(h * half + c * (half // 2), half // 2)
                result = dot(act, ref["down"][:, columns]).astype(BF16)
                store(h, c, result.reshape(2, UNIT, half // 2))

    made_same, made_cross = ref["made_same"], ref["made_cross"]

    def same_experts(yo):
        def load(h):
            return got_same[:, yo, :, pl.ds(h * half, half)].reshape(both, half)

        def store(h, c, value):
            made_same[:, yo, :, pl.ds(h * half + c * (half // 2), half // 2)] = value

        experts(load, store)

    def cross_experts(zz):
        def load(h):
            return got_cross[pl.ds(zz * 4 + 2 * h, 2)].reshape(both, half)

        def store(h, c, value):
            made_cross[pl.ds(zz * 4 + 2 * h, 2), :, pl.ds(c * (half // 2), half // 2)] = value

        experts(load, store)

    def arrived(block, sem):
        pltpu.make_async_copy(block, block, sem).wait()

    def column_step(d):
        yo = (y + 4 - d) % 4
        for q in range(2):
            arrived(got_same.at[q, yo], ref["near"].at[1, d - 1, q])
        same_experts(yo)
        for q in range(2):
            sent.append(
                send(
                    made_same.at[q, yo],
                    back_same.at[role, y],
                    ref["back"].at[0, d - 1, q],
                    ref["back"].at[1, d - 1, role],
                    device(q, zh, yo, z, x),
                )
            )

    core.wait_recv()
    same_experts(y)
    core_back = send(
        made_same.at[1 - role, y],
        back_same.at[role, y],
        ref["core"].at[2],
        ref["core"].at[3],
        device(1 - role, zh, y, z, x),
    )
    own_back = pltpu.make_async_copy(made_same.at[role, y], back_same.at[role, y], ref["core"].at[4])
    own_back.start()

    for d in (1, 3, 2):
        yo = (y + d) % 4
        for q in range(2):
            pick_into(same.at[q, yo], owner_of(q, yo))
            sent.append(
                send(
                    same.at[q, yo],
                    got_same.at[role, y],
                    ref["near"].at[0, d - 1, q],
                    ref["near"].at[1, d - 1, role],
                    device(q, zh, yo, z, x),
                )
            )

    gather = PlaneGather(here, got_cross, lane_half, *[ref[f"c{i}"] for i in range(6)], ls=ref["relay"])
    sums = PlaneSum(here, made_cross, lane_half, *[ref[f"d{i}"] for i in range(11)], own_first=True)

    def cross_step(i):
        gather.complete(i)
        cross_experts(gather.order[i])

    for h in range(2):
        swaps[h].wait_recv()
        gather.begin((h,))
    gather.pass_on(0)
    gather.start(1)
    gather.pass_on(1)
    gather.start(2)
    gather.relay()
    cross_step(0)
    sums.begin(0)
    gather.pass_on(2)
    gather.start(3)
    cross_step(1)
    sums.middle(0)
    gather.pass_on(3)
    column_step(1)
    cross_step(2)
    sums.begin(1)
    column_step(3)
    cross_step(3)
    sums.begin(2)
    sums.middle(1)
    sums.begin(3)
    column_step(2)
    sums.end(1)
    sums.middle(2)
    sums.end(2)
    sums.middle(3)
    sums.end(0)
    sums.end(3)
    for h in range(2):
        at = pl.ds(h * (half // 2), half // 2)
        ref["done"][:, at] = sums.total(h).astype(BF16)
        swaps.append(
            send(ref["done"].at[:, at], ref["back_cross"].at[:, at], ref["swap"].at[2, h], ref["swap"].at[3, h], source)
        )

    core_back.wait_recv()
    own_back.wait()
    for d in (1, 3, 2):
        for q in range(2):
            arrived(back_same.at[q, (y + d) % 4], ref["back"].at[1, d - 1, q])
    swaps[2].wait_recv()
    swaps[3].wait_recv()
    branches = ref["branches"]
    last = PlaneSum(here, branches, flat_half, *[ref[f"e{i}"] for i in range(11)])

    def combine(i):
        zz = last.order[i]
        start = 0
        for size in (256, 256, 384):
            at = pl.ds(pl.multiple_of(zz * quarter + start, 128), size)
            table = back_same[:, :, :, at].reshape(8 * UNIT, size)
            value = dot(ref["shared_act"][...], ref["shared_out"][:, at])
            value = value + dot(ref["gate_high"][...], table) + dot(ref["gate_low"][...], table)
            table = ref["back_cross"][:, pl.ds(pl.multiple_of((zz % 2) * quarter + start, 128), size)]
            routed = dot(ref["cross_high"][...], table) + dot(ref["cross_low"][...], table)
            value = value + jnp.where(cross_half == zz // 2, routed, 0.0)
            branches[at, :] = value.T.astype(BF16)
            start += size
        last.begin(i)

    combine(0)
    combine(1)
    last.middle(0)
    combine(2)
    last.middle(1)
    combine(3)
    last.end(0)
    last.middle(2)
    last.end(1)
    last.middle(3)
    last.end(2)
    last.end(3)
    for h in range(2):
        value = last.total(h) + flat_half(hidden, mine, h)[...].astype(F32)
        out[pl.ds(h * step, step), :] = value.astype(BF16)

    for one in (first, sums, last):
        one.drain()
    gather.finish()
    for one in sent + swaps + [core, core_back]:
        one.wait_send()


def layer_scratch(rows, width, heads_width, units, tp_count):
    half, part = width // 2, width // tp_count
    small, large = (part // 2, rows), (UNIT, half // 2)
    dma, vmem = pltpu.SemaphoreType.DMA, pltpu.VMEM
    named = {
        "gate": vmem((2 * units, width), BF16),
        "up": vmem((2 * units, width), BF16),
        "down": vmem((2 * units, width), BF16),
        "shared_in": vmem((2, units, width), BF16),
        "shared_out": vmem((units, width), BF16),
        "load": dma((16,)),
        "routes": vmem((TOPK, 1, rows), jnp.int32),
        "gates": vmem((TOPK, 1, rows), F32),
        "lengths": vmem((1, rows), jnp.int32),
        "queries": vmem((rows, heads_width), BF16),
        "kv": vmem((rows * L, 2 * HD), BF16),
        "resid": vmem((part, rows), BF16),
        "out_proj": vmem((heads_width, width), BF16),
        "context": vmem((rows, heads_width), BF16),
        "attended": vmem((width, rows), BF16),
        "hidden": vmem((width, rows), BF16),
        "normed": vmem((rows, width), BF16),
        "cross": vmem((UNIT, half), BF16),
        "got_cross": vmem((tp_count, UNIT, half), BF16),
        "made_cross": vmem((tp_count, UNIT, half), BF16),
        "done": vmem((UNIT, half), BF16),
        "back_cross": vmem((UNIT, half), BF16),
        "same": vmem((2, 4, UNIT, width), BF16),
        "got_same": vmem((2, 4, UNIT, width), BF16),
        "made_same": vmem((2, 4, UNIT, width), BF16),
        "back_same": vmem((2, 4, UNIT, width), BF16),
        "weights": vmem((8 * UNIT, rows), F32),
        "gate_high": vmem((rows, 8 * UNIT), BF16),
        "gate_low": vmem((rows, 8 * UNIT), BF16),
        "cross_high": vmem((rows, UNIT), BF16),
        "cross_low": vmem((rows, UNIT), BF16),
        "shared_act": vmem((rows, units), BF16),
        "branches": vmem((width, rows), BF16),
        "swap": dma((4, 2)),
        "relay": dma((2,)),
        "near": dma((2, 3, 2)),
        "back": dma((2, 3, 2)),
        "core": dma((5,)),
    }
    for letter, some in (
        ("a", plane_sum_scratch(small)),
        ("b", plane_gather_scratch()),
        ("c", plane_gather_scratch()),
        ("d", plane_sum_scratch(large)),
        ("e", plane_sum_scratch(small)),
    ):
        named.update({f"{letter}{i}": one for i, one in enumerate(some)})
    return list(named), list(named.values())


def body(
    residual,
    queries,
    kv_cache,
    cache_lengths,
    out_proj,
    norm_gain,
    routes,
    gate_weights,
    expert_in,
    expert_out,
    shared_in,
    shared_out,
):
    rows = residual.shape[1]
    part = residual.shape[2]
    tp_count = lax.axis_size("tp")
    width = part * tp_count
    heads_width = queries.shape[2]

    names, scratch = layer_scratch(rows, width, heads_width, expert_out.shape[1], tp_count)
    vmem, hbm = pl.BlockSpec(memory_space=pltpu.VMEM), pl.BlockSpec(memory_space=pltpu.HBM)
    layer_out = pl.pallas_call(
        functools.partial(layer_kernel, names),
        out_shape=jax.ShapeDtypeStruct((part, rows), BF16),
        in_specs=[vmem] + [hbm] * 11,
        out_specs=vmem,
        scratch_shapes=scratch,
        compiler_params=pltpu.CompilerParams(collective_id=1, has_side_effects=True, vmem_limit_bytes=VMEM_LIMIT),
    )(
        norm_gain,
        cache_lengths.reshape(1, rows),
        jnp.transpose(routes.reshape(1, rows, TOPK), (2, 0, 1)),
        jnp.transpose(gate_weights.reshape(1, rows, TOPK), (2, 0, 1)),
        queries.reshape(rows, heads_width),
        kv_cache.reshape(rows * L, 2 * HD),
        residual.reshape(rows, part).T,
        out_proj,
        expert_in,
        expert_out,
        shared_in,
        shared_out,
    )
    return layer_out.T.reshape(1, rows, part)


def solution(mesh):
    in_specs = (
        P("role", "grp", "tp"),
        P("role", "grp", "tp"),
        P("role", "grp", None, None),
        P("role", "grp"),
        P("tp", None),
        P(),
        P("role", "grp", None),
        P("role", "grp", None),
        P(("role", "grp"), None, "tp", None),
        P(("role", "grp"), "tp", None),
        P(None, "tp", None),
        P("tp", None),
    )
    out_specs = P("role", "grp", "tp")
    return jax.shard_map(body, mesh=mesh, in_specs=in_specs, out_specs=out_specs, check_vma=False)
```

```python
import functools

import jax
import jax.numpy as jnp
from jax import lax
from jax.experimental import pallas as pl
from jax.experimental.pallas import tpu as pltpu
from jax.sharding import PartitionSpec as P

HD = 128
EXPERTS = 32
TOPK = 3
L = 16
CAP = 24
UNIT = 2 * CAP
MESH = pl.DeviceIdType.MESH
BF16 = jnp.bfloat16
F32 = jnp.float32
VMEM_LIMIT = 63 * 1024 * 1024


def places():
    role, grp, tp = lax.axis_index("role"), lax.axis_index("grp"), lax.axis_index("tp")
    return role, grp // 4, grp % 4, tp // 4, tp % 4


def flip(a, b):
    return (a + b) % 2


def xor4(a, b):
    return 2 * flip(a // 2, b // 2) + flip(a % 2, b % 2)


def z_mates(z):
    return {1: xor4(z, 1), 2: (z + 2) % 4, 3: 3 - z}


def device(role, zh, y, z, x):
    return {"role": role, "grp": zh * 4 + y, "tp": z * 4 + x}


def partners(role, zh, y, z, x):
    there = (flip(role, x % 2), 1 - zh)
    return device(*there, xor4(y, z), 3 - z, x), device(*there, xor4(y, 3 - z), 3 - z, x)


def plane_mates(role, zh, y, z, x):
    mates = [device(role, zh, y, z, (x + 1) % 4), device(role, zh, y, z, (x + 3) % 4)]
    return mates + [device(role, zh, y, one, x) for one in z_mates(z).values()]


def column_mates(role, zh, y, z, x):
    mates = [device(one, zh, (y + step) % 4, z, x) for step in (1, 2, 3) for one in (0, 1)]
    return mates + [device(1 - role, zh, y, z, x)]


def remote(src, dst, send_sem, recv_sem, to):
    return pltpu.make_async_remote_copy(
        src_ref=src, dst_ref=dst, send_sem=send_sem, recv_sem=recv_sem, device_id=to, device_id_type=MESH
    )


def send(src, dst, send_sem, recv_sem, to):
    copy = remote(src, dst, send_sem, recv_sem, to)
    copy.start()
    return copy


class PlaneSum:
    def __init__(self, here, part, half, rx1, tx, rx2, zt, zrx, s1, r1, s2, r2, zs, zr, own_first=False):
        self.here, self.part, self.half = here, part, half
        self.rx1, self.tx, self.rx2, self.zt, self.zrx = rx1, tx, rx2, zt, zrx
        self.s1, self.r1, self.s2, self.r2, self.zs, self.zr = s1, r1, s2, r2, zs, zr
        role, zh, y, z, x = here
        mates = z_mates(z)
        self.order = [z, mates[2], mates[3], mates[1]] if own_first else [mates[2], mates[3], mates[1], z]
        self.own = 0 if own_first else 3
        self.zslot = {i: n for n, i in enumerate(i for i in range(4) if i != self.own)}
        self.right, self.left = (x + 1) % 4, (x + 3) % 4
        self.to_right = device(role, zh, y, z, self.right)
        self.to_left = device(role, zh, y, z, self.left)
        self.copies = []
        self.first, self.second, self.zcopies = {}, {}, {}

    def begin(self, i):
        x = self.here[4]
        far = (x + 2) % 4
        base = self.order[i] * 4
        for d, (to, near) in enumerate(((self.to_right, self.right), (self.to_left, self.left))):
            self.first[i, d] = send(
                self.half(self.part, base + far, d), self.rx1.at[i, d], self.s1.at[i, d], self.r1.at[i, d], to
            )
            self.second[i, d, 1 - d] = send(
                self.half(self.part, base + near, 1 - d),
                self.rx2.at[i, d, 1 - d],
                self.s2.at[i, d, 1 - d],
                self.r2.at[i, d, 1 - d],
                to,
            )

    def middle(self, i):
        base = self.order[i] * 4
        for d, (to, near) in enumerate(((self.to_right, self.right), (self.to_left, self.left))):
            self.first[i, d].wait_recv()
            own = self.half(self.part, base + near, d)[...]
            self.tx[i, d] = (self.rx1[i, d].astype(F32) + own.astype(F32)).astype(BF16)
            self.second[i, d, d] = send(
                self.tx.at[i, d], self.rx2.at[i, d, d], self.s2.at[i, d, d], self.r2.at[i, d, d], to
            )

    def line(self, i, h):
        x = self.here[4]
        own = self.half(self.part, self.order[i] * 4 + x, h)[...].astype(F32)
        return own + self.rx2[i, 0, h].astype(F32) + self.rx2[i, 1, h].astype(F32)

    def end(self, i):
        role, zh, y, z, x = self.here
        n = self.zslot.get(i)
        for h in range(2):
            for d in range(2):
                self.second[i, d, h].wait_recv()
            if i == self.own:
                continue
            self.zt[n, h] = self.line(i, h).astype(BF16)
            self.zcopies[n, h] = send(
                self.zt.at[n, h],
                self.zrx.at[n, h],
                self.zs.at[n, h],
                self.zr.at[n, h],
                device(role, zh, y, self.order[i], x),
            )

    def total(self, h):
        value = self.line(self.own, h)
        for i in range(3):
            self.zcopies[i, h].wait_recv()
            value = value + self.zrx[i, h].astype(F32)
        return value

    def drain(self):
        for copy in list(self.first.values()) + list(self.second.values()) + list(self.zcopies.values()):
            copy.wait_send()

    def whole(self, between=lambda: None):
        for i in range(4):
            self.begin(i)
        self.middle(0)
        self.middle(1)
        between()
        self.end(0)
        self.middle(2)
        self.end(1)
        self.middle(3)
        self.end(2)
        self.end(3)


def plane_sum_scratch(half):
    dma = pltpu.SemaphoreType.DMA
    return [
        pltpu.VMEM((4, 2) + half, BF16),
        pltpu.VMEM((4, 2) + half, BF16),
        pltpu.VMEM((4, 2, 2) + half, BF16),
        pltpu.VMEM((3, 2) + half, BF16),
        pltpu.VMEM((3, 2) + half, BF16),
        dma((4, 2)),
        dma((4, 2)),
        dma((4, 2, 2)),
        dma((4, 2, 2)),
        dma((3, 2)),
        dma((3, 2)),
    ]


class PlaneGather:
    def __init__(self, here, out, half, zs, zr, xs, xr, fs, fr, ls=None):
        self.here, self.out, self.half, self.ls = here, out, half, ls
        self.zs, self.zr, self.xs, self.xr, self.fs, self.fr = zs, zr, xs, xr, fs, fr
        role, zh, y, z, x = here
        mates = z_mates(z)
        self.order = [z, mates[1], mates[2], mates[3]]
        self.inner = ((z + 1) // 2) % 2 == 1
        self.relays = []
        self.to_right = device(role, zh, y, z, (x + 1) % 4)
        self.to_left = device(role, zh, y, z, (x + 3) % 4)
        self.zcopies, self.near, self.far = {}, {}, {}

    def begin(self, halves=(0, 1)):
        role, zh, y, z, x = self.here
        mine = z * 4 + x
        for h in halves:
            self.spread(0, h)
            block = self.half(self.out, mine, h)
            for m in (1, 2, 3):
                copy = remote(
                    block, block, self.zs.at[m - 1, h], self.zr.at[m - 1, h], device(role, zh, y, self.order[m], x)
                )
                self.zcopies[m, h] = copy
                if m == 3 and self.ls is not None:
                    pl.when(self.inner)(copy.start)
                else:
                    copy.start()

    def spread(self, i, h):
        block = self.half(self.out, self.order[i] * 4 + self.here[4], h)
        for d, to in ((h, (self.to_right, self.to_left)[h]), (1 - h, (self.to_right, self.to_left)[1 - h])):
            self.near[i, d, h] = send(block, block, self.xs.at[i, d, h], self.xr.at[i, d, h], to)

    def start(self, i):
        for h in range(2):
            self.zcopies[i, h].wait_recv()
            self.spread(i, h)

    def relay(self):
        role, zh, y, z, x = self.here
        for h in range(2):
            block = self.half(self.out, self.order[2] * 4 + x, h)
            copy = remote(block, block, self.ls.at[h], self.zr.at[2, h], device(role, zh, y, self.order[1], x))
            pl.when(self.inner)(copy.start)
            self.relays.append(copy)

    def pass_on(self, i):
        x = self.here[4]
        base = self.order[i] * 4
        for d, (to, slot) in enumerate(((self.to_right, (x + 3) % 4), (self.to_left, (x + 1) % 4))):
            self.near[i, d, d].wait_recv()
            block = self.half(self.out, base + slot, d)
            self.far[i, d] = send(block, block, self.fs.at[i, d], self.fr.at[i, d], to)

    def complete(self, i):
        for d in range(2):
            self.near[i, d, 1 - d].wait_recv()
            self.far[i, d].wait_recv()

    def finish(self):
        for copies in (self.near, self.far):
            for copy in copies.values():
                copy.wait_send()
        for (m, h), copy in self.zcopies.items():
            if m == 3 and self.ls is not None:
                pl.when(self.inner)(copy.wait_send)
            else:
                copy.wait_send()
        for copy in self.relays:
            pl.when(self.inner)(copy.wait_send)

    def whole(self, between=lambda: None):
        self.begin()
        self.pass_on(0)
        self.start(1)
        between()
        self.start(2)
        self.pass_on(1)
        self.start(3)
        self.pass_on(2)
        self.pass_on(3)
        for i in range(4):
            self.complete(i)
        self.finish()


def plane_gather_scratch():
    dma = pltpu.SemaphoreType.DMA
    return [dma((3, 2)), dma((3, 2)), dma((4, 2, 2)), dma((4, 2, 2)), dma((4, 2)), dma((4, 2))]


def flat_half(ref, slot, h):
    rows = ref.shape[0] // 32
    return ref.at[pl.ds(pl.multiple_of((2 * slot + h) * rows, 16), rows), :]


def lane_half(ref, slot, h):
    width = ref.shape[2] // 2
    return ref.at[slot, :, pl.ds(h * width, width)]


def dot(a, b):
    return jnp.dot(a, b, preferred_element_type=F32)


def dot_rows(a, b):
    return lax.dot_general(a, b, (((1,), (1,)), ((), ())), preferred_element_type=F32)


def split(value):
    high = value.astype(BF16)
    return high, (value - high.astype(F32)).astype(BF16)


def slot_rows(routes):
    count = routes[0].shape[1]
    ids = lax.broadcasted_iota(jnp.int32, (EXPERTS, count), 0)
    named = [ids == one for one in routes]
    chosen = jnp.where(named[0] | named[1] | named[2], 1.0, 0.0).astype(BF16)
    earlier = lax.broadcasted_iota(jnp.int32, (count, count), 0) < lax.broadcasted_iota(jnp.int32, (count, count), 1)
    before = dot(chosen, jnp.where(earlier, 1.0, 0.0).astype(BF16))
    place = [jnp.sum(jnp.where(one, before, 0.0), axis=0, keepdims=True).astype(jnp.int32) for one in named]
    return [routes[k] * CAP + place[k] for k in range(TOPK)]


def unit_hits(slots, owner):
    ids = lax.broadcasted_iota(jnp.int32, (UNIT, slots[0].shape[1]), 0) + owner * UNIT
    return [ids == one for one in slots]


def same_place(count):
    place = [lax.broadcasted_iota(jnp.int32, (count, count), d) for d in range(2)]
    return jnp.where(place[0] == place[1], 1.0, 0.0).astype(BF16)


def attend(queries, kv, lengths, context):
    rows = queries.shape[0]
    block = 32
    place = [lax.broadcasted_iota(jnp.int32, (rows, rows), d) for d in range(2)]
    live = jnp.where(place[0] == place[1], lengths[...].astype(F32), 0.0)
    live = jnp.sum(live, axis=1, keepdims=True).astype(jnp.int32)
    ahead = lax.broadcasted_iota(jnp.int32, (block, block * L), 1) - L * lax.broadcasted_iota(
        jnp.int32, (block, block * L), 0
    )
    parts = [(start, head) for start in range(0, rows, block) for head in range(queries.shape[1] // HD)]
    scores = [
        dot_rows(queries[start : start + block, head * HD : (head + 1) * HD], kv[start * L : (start + block) * L, :HD])
        * HD ** (-0.5)
        for start, head in parts
    ]
    weights = []
    for (start, _), score in zip(parts, scores):
        visible = (ahead >= 0) & (ahead < live[start : start + block])
        score = jnp.where(visible, score, -1e30)
        maximum = jnp.max(score, axis=1, keepdims=True)
        exponent = jnp.where(visible, jnp.exp(score - maximum), 0.0)
        weights.append((exponent / jnp.sum(exponent, axis=1, keepdims=True)).astype(BF16))
    for (start, head), weight in zip(parts, weights):
        values = kv[start * L : (start + block) * L, HD:]
        context[start : start + block, head * HD : (head + 1) * HD] = dot(weight, values).astype(BF16)


def layer_kernel(
    names, gain, len_in, routes_in, gates_in, q_in, kv_in, resid_in, o_proj, w_in, w_out, s_in, s_out, out, *scratch
):
    ref = dict(zip(names, scratch))
    here = places()
    role, zh, y, z, x = here
    mine = z * 4 + x
    rows = routes_in.shape[2]
    width = gain.shape[0]
    half = width // 2
    units = w_in.shape[2]
    up_at = up_place(units)
    to, source = partners(*here)

    queries, kv, resid = ref["queries"], ref["kv"], ref["resid"]
    loads = [
        (len_in, ref["lengths"]),
        (q_in, queries),
        (kv_in, kv),
        (o_proj, ref["out_proj"]),
        (routes_in, ref["routes"]),
        (gates_in, ref["gates"]),
        (resid_in, resid),
    ]
    for j in range(2):
        loads.append((w_in.at[j, 0], ref["gate_up"].at[pl.ds(j * units, units), :]))
        loads.append((w_in.at[j, 1], ref["gate_up"].at[pl.ds(up_at + j * units, units), :]))
        loads.append((w_out.at[j], ref["down"].at[pl.ds(j * units, units), :]))
        loads.append((s_in.at[j], ref["shared_in"].at[j]))
    loads.append((s_out, ref["shared_out"]))
    loads = [pltpu.make_async_copy(a, b, ref["load"].at[i]) for i, (a, b) in enumerate(loads)]
    for one in loads[:4]:
        one.start()
    barrier = pltpu.get_barrier_semaphore()
    mates = plane_mates(*here) + column_mates(*here) + [to, source]
    for one in mates:
        pl.semaphore_signal(barrier, inc=1, device_id=one, device_id_type=MESH)

    for one in loads[4:]:
        one.start()
    unused = up_at - 2 * units
    if unused:
        ref["gate_up"][pl.ds(2 * units, unused), :] = jnp.zeros((unused, width), BF16)


    cross_owner = flip(role, x % 2) * 8 + (1 - zh) * 4 + xor4(y, z)
    cross_half = x // 2

    for one in loads[:3]:
        one.wait()
    attend(queries, kv, ref["lengths"], ref["context"])

    eye = same_place(rows)
    quarter = width // 4
    first = PlaneSum(here, ref["attended"], flat_half, *[ref[f"a{i}"] for i in range(11)])
    loads[3].wait()

    def project(i):
        start = 0
        for size in (256, 256, 384):
            at = pl.ds(pl.multiple_of(first.order[i] * quarter + start, 128), size)
            ref["attended"][at, :] = dot(ref["context"][...], ref["out_proj"][:, at]).T.astype(BF16)
            start += size

    project(0)
    pl.semaphore_wait(barrier, len(mates))
    first.begin(0)
    project(1)
    first.begin(1)
    project(2)
    first.begin(2)
    first.middle(0)
    project(3)
    first.begin(3)

    for one in loads[4:7]:
        one.wait()
    slots = slot_rows([ref["routes"][k] for k in range(TOPK)])
    gate_rows = [ref["gates"][k] for k in range(TOPK)]

    def pick(owner):
        hits = unit_hits(slots, owner)
        return jnp.where(hits[0] | hits[1] | hits[2], 1.0, 0.0).astype(BF16)

    def weigh(owner):
        hits = unit_hits(slots, owner)
        return sum(jnp.where(hits[k], gate_rows[k], 0.0) for k in range(TOPK))

    def owner_of(q, yo):
        return q * 8 + zh * 4 + yo

    for q in range(2):
        for yo in range(4):
            at = pl.ds((q * 4 + yo) * UNIT, UNIT)
            ref["weights"][at, :] = weigh(owner_of(q, yo))
    ref["gate_high"][...], ref["gate_low"][...] = split(ref["weights"][...].T)
    ref["cross_high"][...], ref["cross_low"][...] = split(weigh(cross_owner).T)

    first.middle(1)
    first.end(0)
    first.middle(2)
    first.end(1)
    first.middle(3)
    first.end(2)
    first.end(3)
    hidden = ref["hidden"]
    step = resid.shape[0] // 2
    for h in range(2):
        value = first.total(h) + resid[pl.ds(h * step, step), :].astype(F32)
        flat_half(hidden, mine, h)[...] = value.astype(BF16)
    PlaneGather(here, hidden, flat_half, *[ref[f"b{i}"] for i in range(6)]).whole()

    normed = ref["normed"]
    tile = 256
    square = jnp.zeros((1, rows), F32)
    for i in range(width // tile):
        wide = hidden[pl.ds(i * tile, tile), :].astype(F32)
        square = square + jnp.sum(wide * wide, axis=0, keepdims=True)
    scale = jnp.sum(jnp.where(eye > 0, lax.rsqrt(square / width + 1e-06), 0.0), axis=1, keepdims=True)
    for i in range(width // tile):
        at = pl.ds(i * tile, tile)
        wide = dot_rows(eye, hidden[at, :])
        normed[:, at] = (wide * scale * gain[at].astype(F32).reshape(1, tile)).astype(BF16)

    chosen = pick(cross_owner)
    got_cross = ref["got_cross"]
    swaps = []
    for h in range(2):
        at = pl.ds(h * (half // 2), half // 2)
        from_at = pl.ds(pl.multiple_of(cross_half * half + h * (half // 2), 128), half // 2)
        ref["cross"][:, at] = dot(chosen, normed[:, from_at]).astype(BF16)
        swaps.append(
            send(
                ref["cross"].at[:, at],
                got_cross.at[(3 - z) * 4 + x, :, at],
                ref["swap"].at[0, h],
                ref["swap"].at[1, h],
                to,
            )
        )
    same, got_same, back_same = ref["same"], ref["got_same"], ref["back_same"]
    sent = []

    def pick_into(target, owner):
        chosen = pick(owner)
        for h in range(4):
            at = pl.ds(h * (width // 4), width // 4)
            target[:, at] = dot(chosen, normed[:, at]).astype(BF16)

    pick_into(same.at[1 - role, y], owner_of(1 - role, y))
    core = send(
        same.at[1 - role, y], got_same.at[role, y], ref["core"].at[0], ref["core"].at[1], device(1 - role, zh, y, z, x)
    )
    pick_into(got_same.at[role, y], owner_of(role, y))

    for one in loads[7:]:
        one.wait()

    pre = [dot_rows(normed[...], ref["shared_in"][g]) for g in range(2)]
    ref["shared_act"][...] = (jax.nn.silu(pre[0]) * pre[1]).astype(BF16)

    both = 2 * UNIT
    inner = (lax.broadcasted_iota(jnp.int32, (both, 2 * units), 0) % UNIT) >= CAP
    second = lax.broadcasted_iota(jnp.int32, (both, 2 * units), 1) >= units
    own_expert = jnp.logical_not(jnp.logical_xor(inner, second))

    def experts(load, store):
        at = [pl.ds(h * half, half) for h in range(2)]
        found = [load(h) for h in range(2)]
        pre = sum(dot_rows(found[h], ref["gate_up"][:, at[h]]) for h in range(2))
        gate_pre, up_pre = pre[:, : 2 * units], pre[:, up_at:]
        act = jnp.where(own_expert, jax.nn.silu(gate_pre) * up_pre, 0.0).astype(BF16)
        for h in range(2):
            for c in range(2):
                columns = pl.ds(h * half + c * (half // 2), half // 2)
                result = dot(act, ref["down"][:, columns]).astype(BF16)
                store(h, c, result.reshape(2, UNIT, half // 2))

    made_same, made_cross = ref["made_same"], ref["made_cross"]

    def same_experts(yo):
        def load(h):
            return got_same[:, yo, :, pl.ds(h * half, half)].reshape(both, half)

        def store(h, c, value):
            made_same[:, yo, :, pl.ds(h * half + c * (half // 2), half // 2)] = value

        experts(load, store)

    def cross_experts(zz):
        def load(h):
            return got_cross[pl.ds(zz * 4 + 2 * h, 2)].reshape(both, half)

        def store(h, c, value):
            made_cross[pl.ds(zz * 4 + 2 * h, 2), :, pl.ds(c * (half // 2), half // 2)] = value

        experts(load, store)

    def arrived(block, sem):
        pltpu.make_async_copy(block, block, sem).wait()

    def column_step(d):
        yo = (y + 4 - d) % 4
        for q in range(2):
            arrived(got_same.at[q, yo], ref["near"].at[1, d - 1, q])
        same_experts(yo)
        for q in range(2):
            sent.append(
                send(
                    made_same.at[q, yo],
                    back_same.at[role, y],
                    ref["back"].at[0, d - 1, q],
                    ref["back"].at[1, d - 1, role],
                    device(q, zh, yo, z, x),
                )
            )

    for d in (1, 3, 2):
        yo = (y + d) % 4
        for q in range(2):
            pick_into(same.at[q, yo], owner_of(q, yo))
            sent.append(
                send(
                    same.at[q, yo],
                    got_same.at[role, y],
                    ref["near"].at[0, d - 1, q],
                    ref["near"].at[1, d - 1, role],
                    device(q, zh, yo, z, x),
                )
            )

    core.wait_recv()
    same_experts(y)
    core_back = send(
        made_same.at[1 - role, y],
        back_same.at[role, y],
        ref["core"].at[2],
        ref["core"].at[3],
        device(1 - role, zh, y, z, x),
    )
    own_back = pltpu.make_async_copy(made_same.at[role, y], back_same.at[role, y], ref["core"].at[4])
    own_back.start()

    gather = PlaneGather(here, got_cross, lane_half, *[ref[f"c{i}"] for i in range(6)], ls=ref["relay"])
    sums = PlaneSum(here, made_cross, lane_half, *[ref[f"d{i}"] for i in range(11)], own_first=True)

    def cross_step(i):
        gather.complete(i)
        cross_experts(gather.order[i])

    for h in range(2):
        swaps[h].wait_recv()
        gather.begin((h,))
    gather.pass_on(0)
    gather.start(1)
    gather.pass_on(1)
    gather.start(2)
    gather.relay()
    cross_step(0)
    sums.begin(0)
    gather.pass_on(2)
    gather.start(3)
    cross_step(1)
    sums.middle(0)
    gather.pass_on(3)
    sums.begin(3)
    column_step(1)
    cross_step(2)
    sums.begin(1)
    column_step(3)
    cross_step(3)
    sums.begin(2)
    sums.middle(1)
    column_step(2)
    sums.end(1)
    sums.middle(2)
    sums.end(2)
    sums.middle(3)
    sums.end(0)
    sums.end(3)
    for h in range(2):
        at = pl.ds(h * (half // 2), half // 2)
        ref["done"][:, at] = sums.total(h).astype(BF16)
        swaps.append(
            send(ref["done"].at[:, at], ref["back_cross"].at[:, at], ref["swap"].at[2, h], ref["swap"].at[3, h], source)
        )

    core_back.wait_recv()
    own_back.wait()
    for d in (1, 3, 2):
        for q in range(2):
            arrived(back_same.at[q, (y + d) % 4], ref["back"].at[1, d - 1, q])
    swaps[2].wait_recv()
    swaps[3].wait_recv()
    branches = ref["branches"]
    last = PlaneSum(here, branches, flat_half, *[ref[f"e{i}"] for i in range(11)])

    def combine(i):
        zz = last.order[i]
        start = 0
        for size in (256, 256, 384):
            at = pl.ds(pl.multiple_of(zz * quarter + start, 128), size)
            table = back_same[:, :, :, at].reshape(8 * UNIT, size)
            value = dot(ref["shared_act"][...], ref["shared_out"][:, at])
            value = value + dot(ref["gate_high"][...], table) + dot(ref["gate_low"][...], table)
            table = ref["back_cross"][:, pl.ds(pl.multiple_of((zz % 2) * quarter + start, 128), size)]
            routed = dot(ref["cross_high"][...], table) + dot(ref["cross_low"][...], table)
            value = value + jnp.where(cross_half == zz // 2, routed, 0.0)
            branches[at, :] = value.T.astype(BF16)
            start += size
        last.begin(i)

    combine(0)
    combine(1)
    last.middle(0)
    combine(2)
    last.middle(1)
    combine(3)
    last.end(0)
    last.middle(2)
    last.end(1)
    last.middle(3)
    last.end(2)
    last.end(3)
    for h in range(2):
        value = last.total(h) + flat_half(hidden, mine, h)[...].astype(F32)
        out[pl.ds(h * step, step), :] = value.astype(BF16)

    for one in (first, sums, last):
        one.drain()
    gather.finish()
    for one in sent + swaps + [core, core_back]:
        one.wait_send()


def up_place(units):
    return -(-2 * units // 128) * 128


def layer_scratch(rows, width, heads_width, units, tp_count):
    half, part = width // 2, width // tp_count
    small, large = (part // 2, rows), (UNIT, half // 2)
    dma, vmem = pltpu.SemaphoreType.DMA, pltpu.VMEM
    named = {
        "gate_up": vmem((up_place(units) + 2 * units, width), BF16),
        "down": vmem((2 * units, width), BF16),
        "shared_in": vmem((2, units, width), BF16),
        "shared_out": vmem((units, width), BF16),
        "load": dma((16,)),
        "routes": vmem((TOPK, 1, rows), jnp.int32),
        "gates": vmem((TOPK, 1, rows), F32),
        "lengths": vmem((1, rows), jnp.int32),
        "queries": vmem((rows, heads_width), BF16),
        "kv": vmem((rows * L, 2 * HD), BF16),
        "resid": vmem((part, rows), BF16),
        "out_proj": vmem((heads_width, width), BF16),
        "context": vmem((rows, heads_width), BF16),
        "attended": vmem((width, rows), BF16),
        "hidden": vmem((width, rows), BF16),
        "normed": vmem((rows, width), BF16),
        "cross": vmem((UNIT, half), BF16),
        "got_cross": vmem((tp_count, UNIT, half), BF16),
        "made_cross": vmem((tp_count, UNIT, half), BF16),
        "done": vmem((UNIT, half), BF16),
        "back_cross": vmem((UNIT, half), BF16),
        "same": vmem((2, 4, UNIT, width), BF16),
        "got_same": vmem((2, 4, UNIT, width), BF16),
        "made_same": vmem((2, 4, UNIT, width), BF16),
        "back_same": vmem((2, 4, UNIT, width), BF16),
        "weights": vmem((8 * UNIT, rows), F32),
        "gate_high": vmem((rows, 8 * UNIT), BF16),
        "gate_low": vmem((rows, 8 * UNIT), BF16),
        "cross_high": vmem((rows, UNIT), BF16),
        "cross_low": vmem((rows, UNIT), BF16),
        "shared_act": vmem((rows, units), BF16),
        "branches": vmem((width, rows), BF16),
        "swap": dma((4, 2)),
        "relay": dma((2,)),
        "near": dma((2, 3, 2)),
        "back": dma((2, 3, 2)),
        "core": dma((5,)),
    }
    for letter, some in (
        ("a", plane_sum_scratch(small)),
        ("b", plane_gather_scratch()),
        ("c", plane_gather_scratch()),
        ("d", plane_sum_scratch(large)),
        ("e", plane_sum_scratch(small)),
    ):
        named.update({f"{letter}{i}": one for i, one in enumerate(some)})
    return list(named), list(named.values())


def body(
    residual,
    queries,
    kv_cache,
    cache_lengths,
    out_proj,
    norm_gain,
    routes,
    gate_weights,
    expert_in,
    expert_out,
    shared_in,
    shared_out,
):
    rows = residual.shape[1]
    part = residual.shape[2]
    tp_count = lax.axis_size("tp")
    width = part * tp_count
    heads_width = queries.shape[2]

    names, scratch = layer_scratch(rows, width, heads_width, expert_out.shape[1], tp_count)
    vmem, hbm = pl.BlockSpec(memory_space=pltpu.VMEM), pl.BlockSpec(memory_space=pltpu.HBM)
    layer_out = pl.pallas_call(
        functools.partial(layer_kernel, names),
        out_shape=jax.ShapeDtypeStruct((part, rows), BF16),
        in_specs=[vmem] + [hbm] * 11,
        out_specs=vmem,
        scratch_shapes=scratch,
        compiler_params=pltpu.CompilerParams(collective_id=1, has_side_effects=True, vmem_limit_bytes=VMEM_LIMIT),
    )(
        norm_gain,
        cache_lengths.reshape(1, rows),
        jnp.transpose(routes.reshape(1, rows, TOPK), (2, 0, 1)),
        jnp.transpose(gate_weights.reshape(1, rows, TOPK), (2, 0, 1)),
        queries.reshape(rows, heads_width),
        kv_cache.reshape(rows * L, 2 * HD),
        residual.reshape(rows, part).T,
        out_proj,
        expert_in,
        expert_out,
        shared_in,
        shared_out,
    )
    return layer_out.T.reshape(1, rows, part)


def solution(mesh):
    in_specs = (
        P("role", "grp", "tp"),
        P("role", "grp", "tp"),
        P("role", "grp", None, None),
        P("role", "grp"),
        P("tp", None),
        P(),
        P("role", "grp", None),
        P("role", "grp", None),
        P(("role", "grp"), None, "tp", None),
        P(("role", "grp"), "tp", None),
        P(None, "tp", None),
        P("tp", None),
    )
    out_specs = P("role", "grp", "tp")
    return jax.shard_map(body, mesh=mesh, in_specs=in_specs, out_specs=out_specs, check_vma=False)
```
